512 devices in a mesh: seq: 128 (over y, z, core), mp: 4 (over x).
Axes of the slice: x: 4, y: 8, z: 8, core: 2. Of those that a mesh axis runs over, the one named last changes fastest.
Arguments:
- owned_rows: bfloat16 [16384, 2304], P('seq'), may hold values from -6 to 6
- arrival: int32 [128, 128], P('seq'), may hold values from 0 to 127, each once within a row
- image_lengths: int32 [256], replicated, may hold values from 1 to 384, 16384 in all
- probe_seeds: int32 [256], replicated, may hold values from 0 to 999999
- in_gain: float32 [2304], replicated, may hold values from 0.1 to 1.9
- w_q: bfloat16 [2304, 2304], P('seq', 'mp')
- w_kv: bfloat16 [2304, 2, 768], P('seq', None, 'mp')
- w_out: bfloat16 [2304, 2304], P('mp', 'seq'), may hold values from -0.125 to 0.125
Outputs:
- velocity: bfloat16 [16384, 2304], P('seq', 'mp')
- divergence: float32 [256], replicated
The draws below stay inside these ranges and needn't reach their ends.
Inputs may be any that keep to these rules, and one draw needn't show every extreme that they name: Each row of arrival holds every number of 0 to 127 once. `image_lengths`: the lengths sum to 16384; the longest is exactly 384.
All inputs are finite; a program needn't handle non-finite values.
Results may differ from the reference program's by a relative error of at most 0.015.
Values may be sent and summed in bfloat16 or wider, within the bound.
No kernel may reach another device: no remote copies, remote signals or barrier semaphores. Data moves between devices by JAX's collectives and lax.ppermute only.
A program may use at most 64 MiB of HBM per device.

```python
import math
import jax
import jax.numpy as jnp
import numpy as np
from jax import lax

D = 2304
HEADS = 24
KV_HEADS = 8
HEAD_DIM = 96
ROW_DEV = 128
SPAN = 3
SHARDS = 128
TOKENS = 16384
LMAX = 384
IMAGES = 256
N_SEQ = 128
N_MP = 4


def draw_w_q(key, part):
    key = jax.random.fold_in(key, 11)
    base = jax.random.normal(key, (D, HEADS * HEAD_DIM), jnp.float32) / jnp.sqrt(jnp.float32(D))
    return base.astype(jnp.bfloat16)


def draw_w_kv(key, part):
    key = jax.random.fold_in(key, 13)
    base = jax.random.normal(key, (D, 2, KV_HEADS * HEAD_DIM), jnp.float32) / jnp.sqrt(jnp.float32(D))
    return base.astype(jnp.bfloat16)


def touch_ends(entries, key, low, high):
    longest = entries.shape.index(max(entries.shape))
    spots = []
    for shift in (0, 1):
        where = [jax.random.randint(jax.random.fold_in(key, axis), (), 0, length) for axis, length in enumerate(entries.shape)]
        where[longest] = (where[longest] + shift) % entries.shape[longest]
        spots.append(tuple(where))
    return entries.at[spots[0]].set(low).at[spots[1]].set(high)


def levels(key, dims, pieces, least, top_value):
    level = 1.0
    for dim, parts in pieces:
        heights = jax.random.uniform(jax.random.fold_in(jax.random.fold_in(key, 6), dim), (parts,), jnp.float32, least / len(pieces), top_value / len(pieces))
        level = level * jnp.repeat(jnp.exp(heights), dims[dim] // parts).reshape((-1,) + (1,) * (len(dims) - 1 - dim))
    return level


def split_up(number_of, total, limit, lean):
    portions = [(1 << 20) // math.isqrt(rank ** lean) + 1 for rank in range(2, number_of + 1)]
    rest, given = total - limit - (number_of - 1), [1] * (number_of - 1)
    while rest > 0:
        movable = [i for i in range(number_of - 1) if given[i] < limit]
        whole, left = sum([portions[i] for i in movable]), rest
        for i in movable:
            more = min(limit - given[i], max(1, left * portions[i] // whole), rest)
            given[i] = given[i] + more
            rest = rest - more
    return np.array([limit] + given)


def uneven(key, count, total, bound, slope):
    if count == 2:
        one = jax.random.randint(key, (), max(1, total - bound), min(bound, total - 1) + 1)
        return jnp.stack([one, total - one])
    lengths = jnp.asarray(split_up(count, total, bound, slope), jnp.int32)
    pairs = (count - 1) // 2
    source_of, sink = lengths[1:1 + 2 * pairs:2], lengths[2:2 + 2 * pairs:2]
    room = jnp.minimum(source_of - 1, bound - sink)
    passed = jax.random.randint(jax.random.fold_in(key, 1), (pairs,), 0, 1 << 20) % (room + 1)
    lengths = lengths.at[1:1 + 2 * pairs:2].set(source_of - passed).at[2:2 + 2 * pairs:2].set(sink + passed)
    return lengths[jax.random.permutation(jax.random.fold_in(key, 2), count)]


def centred(rng, shape, deviation, most, cuts=(), held_as=jnp.bfloat16):
    factor_of = levels(rng, shape, cuts, -0.22, 0.18) if cuts else 1.0
    entries = jax.random.normal(rng, shape, jnp.float32) * deviation * factor_of
    return jnp.minimum(jnp.maximum(entries, -most), most).astype(held_as)


def setup_inputs(seed: int = 0) -> dict:
    key_list = jax.random.split(jax.random.key(seed), 9)
    return {
        "owned_rows": centred(key_list[0], (TOKENS, D), 1.0, 6.0, ((0, 128),)),
        "arrival": jax.vmap(lambda own: jax.random.permutation(own, ROW_DEV))(jax.random.split(key_list[1], SHARDS)).reshape((SHARDS, ROW_DEV)).astype(jnp.int32),
        "image_lengths": uneven(key_list[2], IMAGES, TOKENS, LMAX, 2).astype(jnp.int32),
        "probe_seeds": touch_ends(jax.random.randint(key_list[3], (IMAGES,), 0, 1000000), jax.random.fold_in(key_list[3], 1), 0, 999999).astype(jnp.int32),
        "in_gain": jnp.clip(1.0 + 0.18 * jax.random.normal(key_list[4], (D,), jnp.float32), 0.1, 1.9),
        "w_q": draw_w_q(jax.random.fold_in(key_list[8], 71), 0),
        "w_kv": draw_w_kv(jax.random.fold_in(key_list[8], 71), 0),
        "w_out": centred(key_list[7], (HEADS * HEAD_DIM, D), (HEADS * HEAD_DIM) ** -0.5, 0.125, ((0, 4), (1, 128))),
    }


def segment_of(pos, ends):
    return lax.optimization_barrier(jnp.sum((ends[None, :] <= pos[:, None]).astype(jnp.int32), axis=1, dtype=jnp.int32))

def image_lookup(pos, image_lengths, probe_seeds):
    ends = jnp.cumsum(image_lengths, dtype=jnp.int32)
    starts = ends - image_lengths
    seg = segment_of(pos, ends)
    onehot = seg[:, None] == jnp.arange(image_lengths.shape[0], dtype=jnp.int32)[None, :]
    start_row = lax.optimization_barrier(jnp.sum(jnp.where(onehot, starts[None, :], 0), axis=1, dtype=jnp.int32))
    seed_row = lax.optimization_barrier(jnp.sum(jnp.where(onehot, probe_seeds[None, :], 0), axis=1, dtype=jnp.int32))
    return (seg, pos - start_row, seed_row, ends)

def probe_signs(seed_row, local_row, width):
    columns = jnp.arange(width, dtype=jnp.int32)
    mixed = seed_row[:, None] * 40503 + local_row[:, None] * 69069 + columns[None, :] * 2654435
    mixed = mixed ^ jnp.right_shift(mixed, 15)
    mixed = mixed * 1597334677
    mixed = mixed ^ jnp.right_shift(mixed, 13)
    mixed = mixed * 668265263
    bit = jnp.right_shift(mixed, 11) & 1
    return (1 - 2 * bit).astype(jnp.float32)

def normalize(packed, signs, in_gain):
    xf = packed.astype(jnp.float32)
    inv = lax.rsqrt(lax.optimization_barrier(jnp.mean(xf * xf, axis=1, keepdims=True)) + 1e-06)
    along = lax.optimization_barrier(jnp.mean(xf * signs, axis=1, keepdims=True))
    h = (xf * inv * in_gain).astype(jnp.bfloat16)
    h_t = ((signs * inv - xf * inv * inv * inv * along) * in_gain).astype(jnp.bfloat16)
    return (h, h_t)

def attend(qh, kh, vh, qth, kth, vth, mask, head_dim):
    scale = 1.0 / head_dim ** 0.5
    scores = jnp.dot(qh, kh.T, preferred_element_type=jnp.float32) * scale
    scores = jnp.where(mask, scores, -1e+30)
    top = lax.optimization_barrier(jnp.max(scores, axis=1, keepdims=True))
    expo = jnp.exp(scores - top)
    probs = expo / lax.optimization_barrier(jnp.sum(expo, axis=1, keepdims=True))
    tangent = (jnp.dot(qth, kh.T, preferred_element_type=jnp.float32) + jnp.dot(qh, kth.T, preferred_element_type=jnp.float32)) * scale
    tangent = jnp.where(mask, tangent, 0.0)
    probs_t = probs * (tangent - lax.optimization_barrier(jnp.sum(probs * tangent, axis=1, keepdims=True)))
    pb = probs.astype(jnp.bfloat16)
    ptb = probs_t.astype(jnp.bfloat16)
    out = jnp.dot(pb, vh, preferred_element_type=jnp.float32).astype(jnp.bfloat16)
    out_t = (jnp.dot(ptb, vh, preferred_element_type=jnp.float32) + jnp.dot(pb, vth, preferred_element_type=jnp.float32)).astype(jnp.bfloat16)
    return (out, out_t)

def reference(owned_rows, arrival, image_lengths, probe_seeds, in_gain, w_q, w_kv, w_out):
    quota = ROW_DEV // N_SEQ
    shard_ids = jnp.arange(SHARDS, dtype=jnp.int32)[:, None]
    owner = arrival // quota * ROW_DEV + shard_ids * quota + arrival % quota
    packed = jnp.take(owned_rows, owner.reshape(-1), axis=0)
    positions = jnp.arange(TOKENS, dtype=jnp.int32)
    seg, local, seed_row, ends = image_lookup(positions, image_lengths, probe_seeds)
    signs = probe_signs(seed_row, local, D)
    h, h_t = normalize(packed, signs, in_gain)
    both = jnp.concatenate([h, h_t], axis=0)
    proj_q = jnp.dot(both, w_q, preferred_element_type=jnp.float32).astype(jnp.bfloat16)
    proj_k = jnp.dot(both, w_kv[:, 0], preferred_element_type=jnp.float32).astype(jnp.bfloat16)
    proj_v = jnp.dot(both, w_kv[:, 1], preferred_element_type=jnp.float32).astype(jnp.bfloat16)
    query, query_t = (proj_q[:TOKENS], proj_q[TOKENS:])
    stacked = jnp.stack([proj_k[:TOKENS], proj_v[:TOKENS], proj_k[TOKENS:], proj_v[TOKENS:]])
    margin = SPAN * ROW_DEV
    padded = jnp.pad(stacked, ((0, 0), (margin, margin), (0, 0)))
    reach = (2 * SPAN + 1) * ROW_DEV
    group_size = HEADS // KV_HEADS

    def block(index):
        start = index * ROW_DEV
        window = lax.dynamic_slice_in_dim(padded, start, reach, 1)
        qb = lax.dynamic_slice_in_dim(query, start, ROW_DEV, 0)
        qtb = lax.dynamic_slice_in_dim(query_t, start, ROW_DEV, 0)
        qpos = start + jnp.arange(ROW_DEV, dtype=jnp.int32)
        kpos = start - margin + jnp.arange(reach, dtype=jnp.int32)
        valid = (kpos >= 0) & (kpos < TOKENS)
        mask = (segment_of(qpos, ends)[:, None] == segment_of(kpos, ends)[None, :]) & valid[None, :]
        outs, outs_t = ([], [])
        for head in range(HEADS):
            lo = head * HEAD_DIM
            hi = lo + HEAD_DIM
            klo = head // group_size * HEAD_DIM
            khi = klo + HEAD_DIM
            out, out_t = attend(qb[:, lo:hi], window[0, :, klo:khi], window[1, :, klo:khi], qtb[:, lo:hi], window[2, :, klo:khi], window[3, :, klo:khi], mask, HEAD_DIM)
            outs.append(out)
            outs_t.append(out_t)
        return (jnp.concatenate(outs, axis=1), jnp.concatenate(outs_t, axis=1))
    attended, attended_t = lax.map(block, jnp.arange(SHARDS, dtype=jnp.int32))
    attended = attended.reshape(TOKENS, HEADS * HEAD_DIM)
    attended_t = attended_t.reshape(TOKENS, HEADS * HEAD_DIM)
    group = HEADS * HEAD_DIM // N_MP
    total = jnp.zeros((TOKENS, D), jnp.float32)
    total_t = jnp.zeros((TOKENS, D), jnp.float32)
    for index in range(N_MP):
        lo = index * group
        weight = w_out[lo:lo + group]
        part = jnp.dot(attended[:, lo:lo + group], weight, preferred_element_type=jnp.float32)
        part_t = jnp.dot(attended_t[:, lo:lo + group], weight, preferred_element_type=jnp.float32)
        part = lax.optimization_barrier(part.astype(jnp.bfloat16)).astype(jnp.float32)
        part_t = lax.optimization_barrier(part_t.astype(jnp.bfloat16)).astype(jnp.float32)
        total = total + part
        total_t = total_t + part_t
    velocity = total.astype(jnp.bfloat16)
    row_terms = lax.optimization_barrier(jnp.sum(total_t * signs, axis=1))
    divergence = jax.ops.segment_sum(row_terms, seg, num_segments=IMAGES) / D
    return (velocity, divergence)
```

```python
import functools

import jax
import jax.numpy as jnp
from jax import lax
from jax.experimental import pallas as pl
from jax.experimental.pallas import tpu as pltpu
from jax.sharding import Mesh
from jax.sharding import PartitionSpec as P

HEADS = 24
KV_HEADS = 8
HEAD_DIM = 96
GROUP = HEADS // KV_HEADS
SPAN = 3
SEQ = ("y", "z", "c")
COLUMN = ("y", "z")
TILE = ("c", "x")


def segment_of(pos, ends):
    return jnp.sum((ends[None, :] <= pos[:, None]).astype(jnp.int32), axis=1, dtype=jnp.int32)


def probe_signs(seed_row, local_row, width):
    columns = jnp.arange(width, dtype=jnp.int32)
    mixed = seed_row[:, None] * 40503 + local_row[:, None] * 69069 + columns[None, :] * 2654435
    mixed = mixed ^ jnp.right_shift(mixed, 15)
    mixed = mixed * 1597334677
    mixed = mixed ^ jnp.right_shift(mixed, 13)
    mixed = mixed * 668265263
    bit = jnp.right_shift(mixed, 11) & 1
    return (1 - 2 * bit).astype(jnp.float32)


def normalize(packed, signs, in_gain):
    xf = packed.astype(jnp.float32)
    inv = lax.rsqrt(jnp.mean(xf * xf, axis=1, keepdims=True) + 1e-06)
    along = jnp.mean(xf * signs, axis=1, keepdims=True)
    h = (xf * inv * in_gain).astype(jnp.bfloat16)
    h_t = ((signs * inv - xf * inv * inv * inv * along) * in_gain).astype(jnp.bfloat16)
    return (h, h_t)


def spread(array, axes):
    count = lax.axis_size(axes)
    copies = jnp.broadcast_to(array[None], (count,) + array.shape)
    return lax.all_to_all(copies, axes, split_axis=0, concat_axis=0, tiled=True)


def moved(array, by):
    count = lax.axis_size(COLUMN)
    pairs = [(i, i + by) for i in range(count) if 0 <= i + by < count]
    return lax.ppermute(array, COLUMN, pairs)


NT = (((1,), (1,)), ((), ()))


def attend_kernel(
    rows, q_ref, far_before, before, here, after, far_after, segq_ref, segk_ref, u_ref, w_any,
    part_ref, share_ref, window, weight, o_ext, w_sem,
):
    block = 2 * rows
    reach = (2 * SPAN + 1) * rows
    q_width = GROUP * HEAD_DIM
    o_width = weight.shape[1]
    fetch = pltpu.make_async_copy(w_any.at[:, pl.ds(w_any.shape[1] - o_width, o_width)], weight, w_sem)
    fetch.start()
    window[0:rows] = far_before[...]
    window[rows : rows + block] = before[...]
    window[rows + block : rows + 2 * block] = here[...]
    window[rows + 2 * block : rows + 3 * block] = after[...]
    window[rows + 3 * block : 2 * rows + 3 * block] = far_after[...]
    scale = 1.0 / HEAD_DIM**0.5
    to_exp2 = scale * 1.4426950408889634
    row_terms = []
    o_ext[:, : o_width - q_width] = jnp.zeros((block, o_width - q_width), jnp.bfloat16)
    for tile in range(2):
        lo = tile * rows
        keys = window[lo : lo + reach, 0:HEAD_DIM]
        values = window[lo : lo + reach, HEAD_DIM : 2 * HEAD_DIM]
        keys_t = window[lo : lo + reach, 2 * HEAD_DIM : 3 * HEAD_DIM]
        values_t = window[lo : lo + reach, 3 * HEAD_DIM : 4 * HEAD_DIM]
        mask = segq_ref[lo : lo + rows, :] == segk_ref[:, lo : lo + reach]
        terms = jnp.zeros((rows, 1), jnp.float32)
        for head in range(GROUP):
            a, b = head * HEAD_DIM, (head + 1) * HEAD_DIM
            q = q_ref[lo : lo + rows, a:b]
            q_t = q_ref[block + lo : block + lo + rows, a:b]
            s = lax.dot_general(q, keys, NT, preferred_element_type=jnp.float32)
            s_t = lax.dot_general(q_t, keys, NT, preferred_element_type=jnp.float32)
            s_t += lax.dot_general(q, keys_t, NT, preferred_element_type=jnp.float32)
            s = jnp.where(mask, s, -1e30)
            e = jnp.exp2((s - jnp.max(s, axis=1, keepdims=True)) * to_exp2)
            inv = 1.0 / jnp.sum(e, axis=1, keepdims=True)
            mean = jnp.sum(e * s_t, axis=1, keepdims=True) * inv
            e_t = (e * ((s_t - mean) * scale)).astype(jnp.bfloat16)
            e = e.astype(jnp.bfloat16)
            out = jnp.dot(e, values, preferred_element_type=jnp.float32) * inv
            out_t = jnp.dot(e_t, values, preferred_element_type=jnp.float32)
            out_t += jnp.dot(e, values_t, preferred_element_type=jnp.float32)
            out_t = (out_t * inv).astype(jnp.bfloat16).astype(jnp.float32)
            shift = o_width - q_width
            o_ext[lo : lo + rows, shift + a : shift + b] = out.astype(jnp.bfloat16)
            terms += jnp.sum(out_t * u_ref[lo : lo + rows, a:b], axis=1, keepdims=True)
        row_terms.append(terms)
    images = share_ref.shape[1]
    share = jnp.zeros((1, images), jnp.float32)
    for tile in range(2):
        lo = tile * rows
        numbers = lax.broadcasted_iota(jnp.int32, (rows, images), 1)
        hit = segq_ref[lo : lo + rows, :] == numbers
        share += jnp.sum(jnp.where(hit, row_terms[tile], 0.0), axis=0, keepdims=True)
    share_ref[...] = share
    fetch.wait()
    width = weight.shape[0]
    step = width // 6
    for part in range(6):
        a, b = part * step, (part + 1) * step
        part_ref[:, a:b] = lax.dot_general(
            o_ext[...], weight[a:b, :], NT, preferred_element_type=jnp.float32
        ).astype(jnp.bfloat16)


def attend(q, neighbours, segq, segk, u, weights, images):
    block = q.shape[0] // 2
    rows = block // 2
    width, columns = weights.shape
    o_width = 3 * 128
    vmem = pl.BlockSpec(memory_space=pltpu.VMEM)
    return pl.pallas_call(
        functools.partial(attend_kernel, rows),
        out_shape=(
            jax.ShapeDtypeStruct((block, width), jnp.bfloat16),
            jax.ShapeDtypeStruct((1, images), jnp.float32),
        ),
        in_specs=[vmem] * 9 + [pl.BlockSpec(memory_space=pl.ANY)],
        out_specs=(vmem, vmem),
        scratch_shapes=[
            pltpu.VMEM((8 * rows, 4 * HEAD_DIM), jnp.bfloat16),
            pltpu.VMEM((width, o_width), jnp.bfloat16),
            pltpu.VMEM((block, o_width), jnp.bfloat16),
            pltpu.SemaphoreType.DMA,
        ],
        compiler_params=pltpu.CompilerParams(vmem_limit_bytes=40 * 1024 * 1024),
        cost_estimate=pl.CostEstimate(flops=2_000_000_000, bytes_accessed=5_000_000, transcendentals=700_000),
    )(q, *neighbours, segq, segk, u, weights)


def body(owned_rows, arrival, image_lengths, probe_seeds, in_gain, w_q, w_kv, w_out):
    rows, width = owned_rows.shape
    n_x = lax.axis_size("x")
    core, member = lax.axis_index("c"), lax.axis_index("x")
    n_block = lax.axis_size(COLUMN)
    block_index = lax.axis_index(COLUMN)
    quarter = width // n_x
    depth = w_q.shape[0]
    block = 2 * rows
    images = image_lengths.shape[0]

    halves = jnp.concatenate(
        [
            w_q.reshape(depth, 2, -1),
            w_kv[:, 0].reshape(depth, 2, -1),
            w_kv[:, 1].reshape(depth, 2, -1),
            w_out.T.reshape(depth, 2, -1),
        ],
        axis=2,
    )
    halves = jnp.transpose(halves, (1, 0, 2))
    columns = halves.shape[2]
    n_z = lax.axis_size("z")
    pieces = jnp.broadcast_to(halves[None], (n_z,) + halves.shape).reshape(2 * n_z, depth, columns)
    strip = lax.all_to_all(pieces, ("z", "c"), split_axis=0, concat_axis=0, tiled=True)
    strip = strip.reshape(2 * n_z * depth, columns)
    weights = lax.all_gather(strip, "y", axis=0, tiled=True)

    part = lax.dynamic_slice_in_dim(owned_rows, member * quarter, quarter, 1)
    part, strip = lax.optimization_barrier((part, strip))
    arrived = lax.all_to_all(part, SEQ, split_axis=0, concat_axis=0, tiled=True)
    arrived = jnp.take(arrived, arrival[0], axis=0)
    own = lax.all_gather(arrived, "x", axis=1, tiled=True)
    other = lax.ppermute(own, "c", [(0, 1), (1, 0)])
    packed = jnp.concatenate([jnp.where(core == 0, own, other), jnp.where(core == 0, other, own)], axis=0)

    ends = jnp.cumsum(image_lengths, dtype=jnp.int32)
    starts = ends - image_lengths
    first = block_index * block
    positions = first + jnp.arange(block, dtype=jnp.int32)
    seg = segment_of(positions, ends)
    onehot = seg[:, None] == jnp.arange(images, dtype=jnp.int32)[None, :]
    start_row = jnp.sum(jnp.where(onehot, starts[None, :], 0), axis=1, dtype=jnp.int32)
    seed_row = jnp.sum(jnp.where(onehot, probe_seeds[None, :], 0), axis=1, dtype=jnp.int32)
    signs = probe_signs(seed_row, positions - start_row, width)
    kpos = first - SPAN * rows + jnp.arange(block + 2 * SPAN * rows, dtype=jnp.int32)
    valid = (kpos >= 0) & (kpos < block * n_block)
    segk = jnp.where(valid, segment_of(kpos, ends), -1)

    h, h_t = normalize(packed, signs, in_gain)
    stacked = jnp.concatenate([h, h_t, signs.astype(jnp.bfloat16)], axis=0)
    products = jnp.dot(stacked, weights, preferred_element_type=jnp.float32)
    q_width = GROUP * HEAD_DIM
    kv_end = q_width + 2 * HEAD_DIM
    q = products[: 2 * block, :q_width].astype(jnp.bfloat16)
    kv = jnp.concatenate(
        [products[:block, q_width:kv_end], products[block : 2 * block, q_width:kv_end]], axis=1
    ).astype(jnp.bfloat16)
    u = products[2 * block :, kv_end:]

    neighbours = (moved(kv[rows:], 2), moved(kv, 1), kv, moved(kv, -1), moved(kv[:rows], -2))
    partial, share = attend(q, neighbours, seg[:, None], segk[None, :], u, weights, images)

    halves_out = partial.reshape(2, rows, width)
    mine = lax.dynamic_index_in_dim(halves_out, core, 0, keepdims=False)
    theirs = lax.dynamic_index_in_dim(halves_out, 1 - core, 0, keepdims=False)
    theirs = lax.ppermute(theirs, "c", [(0, 1), (1, 0)])
    group = (mine.astype(jnp.float32) + theirs.astype(jnp.float32)).astype(jnp.bfloat16)
    group = jnp.transpose(group.reshape(rows, n_x, quarter), (1, 0, 2))
    groups = lax.all_to_all(group, "x", split_axis=0, concat_axis=0, tiled=True)
    velocity = jnp.sum(groups.astype(jnp.float32), axis=0).astype(jnp.bfloat16)

    share = jnp.sum(spread(share[0], TILE), axis=0)
    share = jnp.sum(spread(share, COLUMN), axis=0)
    divergence = share / width
    return (velocity, divergence)


def solution(mesh):
    n_seq, n_x = mesh.devices.shape
    n_y = 1
    while n_y * n_y * 2 < n_seq:
        n_y *= 2
    devices = mesh.devices.reshape(n_y, n_seq // 2 // n_y, 2, n_x)
    split = Mesh(devices, ("y", "z", "c", "x"))
    in_specs = (
        P(SEQ, None),
        P(SEQ, None),
        P(),
        P(),
        P(),
        P(SEQ, "x"),
        P(SEQ, None, "x"),
        P("x", SEQ),
    )
    out_specs = (P(SEQ, "x"), P())
    return jax.shard_map(body, mesh=split, in_specs=in_specs, out_specs=out_specs, check_vma=False)
```

```python
import functools

import jax
import jax.numpy as jnp
from jax import lax
from jax.experimental import pallas as pl
from jax.experimental.pallas import tpu as pltpu
from jax.sharding import Mesh
from jax.sharding import PartitionSpec as P

HEADS = 24
KV_HEADS = 8
HEAD_DIM = 96
GROUP = HEADS // KV_HEADS
SPAN = 3
SEQ = ("y", "z", "c")
COLUMN = ("y", "z")


def segment_of(pos, ends):
    return jnp.sum((ends[None, :] <= pos[:, None]).astype(jnp.int32), axis=1, dtype=jnp.int32)


def probe_signs(seed_row, local_row, width):
    columns = jnp.arange(width, dtype=jnp.int32)
    mixed = seed_row[:, None] * 40503 + local_row[:, None] * 69069 + columns[None, :] * 2654435
    mixed = mixed ^ jnp.right_shift(mixed, 15)
    mixed = mixed * 1597334677
    mixed = mixed ^ jnp.right_shift(mixed, 13)
    mixed = mixed * 668265263
    bit = jnp.right_shift(mixed, 11) & 1
    return (1 - 2 * bit).astype(jnp.float32)


def spread(array, axes):
    count = lax.axis_size(axes)
    copies = jnp.broadcast_to(array[None], (count,) + array.shape)
    return lax.all_to_all(copies, axes, split_axis=0, concat_axis=0, tiled=True)


def moved(array, by):
    count = lax.axis_size(COLUMN)
    pairs = [(i, i + by) for i in range(count) if 0 <= i + by < count]
    return lax.ppermute(array, COLUMN, pairs)


NT = (((1,), (1,)), ((), ()))
VMEM = pl.BlockSpec(memory_space=pltpu.VMEM)
SMEM = pl.BlockSpec(memory_space=pltpu.SMEM)
ANY = pl.BlockSpec(memory_space=pl.ANY)
LANES = 128


def params(mib):
    return pltpu.CompilerParams(vmem_limit_bytes=mib * 1024 * 1024)


def pack_kernel(depth, wq_ref, wkv_ref, wo_ref, out_ref, wide, tall):
    q_width = GROUP * HEAD_DIM
    kv_width = wkv_ref.shape[1] // 2
    tiles = wide.shape[1] // LANES
    wq = wq_ref[...].astype(jnp.float32)
    wkv = wkv_ref[...].astype(jnp.float32)
    wo = wo_ref[...].astype(jnp.float32)
    tall[...] = jnp.zeros_like(tall)
    for core in range(2):
        k, q = core * HEAD_DIM, core * q_width
        wide[:, :HEAD_DIM] = wkv[:, k : k + HEAD_DIM]
        wide[:, HEAD_DIM : 2 * HEAD_DIM] = wkv[:, kv_width + k : kv_width + k + HEAD_DIM]
        wide[:, 2 * HEAD_DIM : 2 * HEAD_DIM + q_width] = wq[:, q : q + q_width]
        wide[:, 2 * HEAD_DIM + q_width :] = wo[:, q : q + q_width]
        for tile in range(tiles):
            tall[tile * depth : (tile + 1) * depth, :] = wide[:, tile * LANES : (tile + 1) * LANES]
        piece = tall[...].astype(jnp.bfloat16)
        for z in range(out_ref.shape[0] // 2):
            out_ref[2 * z + core] = piece


def unpack_kernel(depth, in_ref, out_ref, tall, wide):
    for source in range(in_ref.shape[0]):
        tall[...] = in_ref[source].astype(jnp.float32)
        for tile in range(out_ref.shape[1] // LANES):
            wide[source * depth : (source + 1) * depth, tile * LANES : (tile + 1) * LANES] = tall[
                tile * depth : (tile + 1) * depth, :
            ]
    out_ref[...] = wide[...].astype(jnp.bfloat16)


def norm_kernel(core_ref, own_ref, other_ref, signs_ref, gain_ref, out_ref, wide):
    rows, width = wide.shape
    quarter = own_ref.shape[1]
    gain = gain_ref[...]
    for half in range(2):
        mine = core_ref[0] == half
        for x in range(width // quarter):
            a, b = x * rows, (x + 1) * rows
            both = jnp.where(mine, own_ref[a:b, :].astype(jnp.float32), other_ref[a:b, :].astype(jnp.float32))
            wide[:, x * quarter : (x + 1) * quarter] = both
        x = wide[...]
        signs = signs_ref[half * rows : (half + 1) * rows, :].astype(jnp.float32)
        inv = lax.rsqrt(jnp.sum(x * x, axis=1, keepdims=True) / width + 1e-06)
        along = jnp.sum(x * signs, axis=1, keepdims=True) / width
        out_ref[half * rows : (half + 1) * rows, :] = (x * inv * gain).astype(jnp.bfloat16)
        out_ref[(2 + half) * rows : (3 + half) * rows, :] = (
            (signs * inv - x * (inv * inv * inv * along)) * gain
        ).astype(jnp.bfloat16)


def kv_kernel(hh_ref, w_any, kv_ref, qa_ref, weight, sem):
    block = kv_ref.shape[0]
    fetch = pltpu.make_async_copy(w_any.at[:, pl.ds(0, 2 * LANES)], weight, sem)
    fetch.start()
    fetch.wait()
    both = 2 * HEAD_DIM
    for part in range(2):
        r = jnp.dot(
            hh_ref[part * block : (part + 1) * block, :], weight[...], preferred_element_type=jnp.float32
        )
        kv_ref[:, part * both : (part + 1) * both] = r[:, :both].astype(jnp.bfloat16)
        qa_ref[part * block : (part + 1) * block, :] = r[:, LANES:].astype(jnp.bfloat16)


def q_kernel(hh_ref, signs_ref, qa_ref, w_any, q_ref, u_ref, weight, sem):
    fetch = pltpu.make_async_copy(w_any.at[:, pl.ds(2 * LANES, 4 * LANES)], weight, sem)
    fetch.start()
    fetch.wait()
    early = 2 * LANES - 2 * HEAD_DIM
    late = q_ref.shape[1] - early
    q_ref[:, :early] = qa_ref[:, LANES - early :]
    r = jnp.dot(hh_ref[...], weight[:, : 2 * LANES], preferred_element_type=jnp.float32)
    q_ref[:, early:] = r[:, :late].astype(jnp.bfloat16)
    u_ref[...] = jnp.dot(signs_ref[...], weight[:, LANES:], preferred_element_type=jnp.float32)


def thirds(total):
    high = total.astype(jnp.bfloat16).astype(jnp.float32)
    middle = (total - high).astype(jnp.bfloat16).astype(jnp.float32)
    low = total - high - middle
    at = lax.broadcasted_iota(jnp.int32, (16, total.shape[1]), 0)
    rest = jnp.where(at == 1, middle, jnp.where(at == 2, low, 0.0))
    return jnp.where(at == 0, high, rest).astype(jnp.bfloat16)


def attend_kernel(
    rows, core_ref, q_ref, far_before, before, here, after, far_after, segq_ref, segk_ref, u_ref, w_any,
    mine_ref, theirs_ref, share_ref, window, weight, o_ext, w_sem,
):
    block = 2 * rows
    reach = (2 * SPAN + 1) * rows
    q_width = GROUP * HEAD_DIM
    o_width = weight.shape[1]
    shift = o_width - q_width
    fetch = pltpu.make_async_copy(w_any.at[:, pl.ds(w_any.shape[1] - o_width, o_width)], weight, w_sem)
    fetch.start()
    window[0:rows] = far_before[...]
    window[rows : rows + block] = before[...]
    window[rows + block : rows + 2 * block] = here[...]
    window[rows + 2 * block : rows + 3 * block] = after[...]
    window[rows + 3 * block : 2 * rows + 3 * block] = far_after[...]
    scale = 1.0 / HEAD_DIM**0.5
    to_exp2 = scale * 1.4426950408889634
    o_ext[:, :shift] = jnp.zeros((block, shift), jnp.bfloat16)
    images = share_ref.shape[1]
    share = jnp.zeros((1, images), jnp.float32)
    for tile in range(2):
        lo = tile * rows
        keys = window[lo : lo + reach, 0:HEAD_DIM]
        values = window[lo : lo + reach, HEAD_DIM : 2 * HEAD_DIM]
        keys_t = window[lo : lo + reach, 2 * HEAD_DIM : 3 * HEAD_DIM]
        values_t = window[lo : lo + reach, 3 * HEAD_DIM : 4 * HEAD_DIM]
        mask = segq_ref[lo : lo + rows, :] == segk_ref[:, lo : lo + reach]
        terms = jnp.zeros((rows, 1), jnp.float32)
        for head in range(GROUP):
            a, b = head * HEAD_DIM, (head + 1) * HEAD_DIM
            q = q_ref[lo : lo + rows, a:b]
            q_t = q_ref[block + lo : block + lo + rows, a:b]
            s = lax.dot_general(q, keys, NT, preferred_element_type=jnp.float32)
            s_t = lax.dot_general(q_t, keys, NT, preferred_element_type=jnp.float32)
            s_t += lax.dot_general(q, keys_t, NT, preferred_element_type=jnp.float32)
            s = jnp.where(mask, s, -1e30)
            e = jnp.exp2((s - jnp.max(s, axis=1, keepdims=True)) * to_exp2)
            inv = 1.0 / jnp.sum(e, axis=1, keepdims=True)
            mean = jnp.sum(e * s_t, axis=1, keepdims=True) * inv
            e_t = (e * ((s_t - mean) * scale)).astype(jnp.bfloat16)
            e = e.astype(jnp.bfloat16)
            out = jnp.dot(e, values, preferred_element_type=jnp.float32) * inv
            out_t = jnp.dot(e_t, values, preferred_element_type=jnp.float32)
            out_t += jnp.dot(e, values_t, preferred_element_type=jnp.float32)
            out_t = (out_t * inv).astype(jnp.bfloat16).astype(jnp.float32)
            o_ext[lo : lo + rows, shift + a : shift + b] = out.astype(jnp.bfloat16)
            terms += jnp.sum(out_t * u_ref[lo : lo + rows, shift + a : shift + b], axis=1, keepdims=True)
        numbers = lax.broadcasted_iota(jnp.int32, (rows, images), 1)
        hit = segq_ref[lo : lo + rows, :] == numbers
        share += jnp.sum(jnp.where(hit, terms, 0.0), axis=0, keepdims=True)
    share_ref[...] = share
    width = weight.shape[0]
    theirs_ref[rows:, :images] = thirds(share)
    theirs_ref[rows:, images:] = jnp.zeros((theirs_ref.shape[0] - rows, width - images), jnp.bfloat16)
    fetch.wait()
    step = width // 6
    core = core_ref[0]
    own = o_ext[pl.ds(pl.multiple_of(core * rows, rows), rows), :]
    other = o_ext[pl.ds(pl.multiple_of((1 - core) * rows, rows), rows), :]
    for part in range(6):
        a, b = part * step, (part + 1) * step
        theirs_ref[:rows, a:b] = lax.dot_general(
            other, weight[a:b, :], NT, preferred_element_type=jnp.float32
        ).astype(jnp.bfloat16)
        mine_ref[:, a:b] = lax.dot_general(own, weight[a:b, :], NT, preferred_element_type=jnp.float32)


def join_kernel(mine_ref, share_ref, theirs_ref, out_ref):
    rows = mine_ref.shape[0]
    images = share_ref.shape[1]
    extra, quarter = out_ref.shape[1] - rows, out_ref.shape[2]
    got = theirs_ref[rows:, :images].astype(jnp.float32)
    share = thirds(share_ref[...] + jnp.sum(got, axis=0, keepdims=True))
    for x in range(out_ref.shape[0]):
        a, b = x * quarter, (x + 1) * quarter
        out_ref[x, :rows, :] = (mine_ref[:, a:b] + theirs_ref[:rows, a:b].astype(jnp.float32)).astype(jnp.bfloat16)
        out_ref[x, rows:, :images] = share
        out_ref[x, rows:, images:] = jnp.zeros((extra, quarter - images), jnp.bfloat16)


def body(owned_rows, arrival, image_lengths, probe_seeds, in_gain, w_q, w_kv, w_out):
    bf16, f32 = jnp.bfloat16, jnp.float32
    rows, width = owned_rows.shape
    n_x, n_z, n_seq = lax.axis_size("x"), lax.axis_size("z"), lax.axis_size(SEQ)
    core, member = lax.axis_index("c"), lax.axis_index("x")
    core_word = jnp.reshape(core, (1,)).astype(jnp.int32)
    n_block = lax.axis_size(COLUMN)
    block_index = lax.axis_index(COLUMN)
    quarter = width // n_x
    depth = w_q.shape[0]
    block = 2 * rows
    images = image_lengths.shape[0]
    q_width = GROUP * HEAD_DIM
    columns = 2 * HEAD_DIM + 2 * q_width

    tall_rows = -(-depth * (columns // LANES) // 16) * 16
    pieces = pl.pallas_call(
        functools.partial(pack_kernel, depth),
        out_shape=jax.ShapeDtypeStruct((2 * n_z, tall_rows, LANES), bf16),
        in_specs=[VMEM] * 3,
        out_specs=VMEM,
        scratch_shapes=[pltpu.VMEM((depth, columns), f32), pltpu.VMEM((tall_rows, LANES), f32)],
        compiler_params=params(16),
    )(w_q, w_kv.reshape(depth, -1), w_out.T)
    strip = lax.all_to_all(pieces, ("z", "c"), split_axis=0, concat_axis=0, tiled=True)
    strip = pl.pallas_call(
        functools.partial(unpack_kernel, depth),
        out_shape=jax.ShapeDtypeStruct((2 * n_z * depth, columns), bf16),
        in_specs=[VMEM],
        out_specs=VMEM,
        scratch_shapes=[pltpu.VMEM((tall_rows, LANES), f32), pltpu.VMEM((2 * n_z * depth, columns), f32)],
        compiler_params=params(16),
    )(strip)
    weights = lax.all_gather(strip, "y", axis=0, tiled=True)

    part = lax.dynamic_slice_in_dim(owned_rows, member * quarter, quarter, 1)
    padded = -(-quarter // LANES) * LANES
    part = jnp.pad(part, ((0, 0), (0, padded - quarter))).reshape(rows, 1, padded)
    part, strip = lax.optimization_barrier((part, strip))
    arrived = lax.all_to_all(part, SEQ, split_axis=0, concat_axis=0, tiled=True)
    arrived = jnp.take(arrived.reshape(rows, padded)[:, :quarter], arrival[0], axis=0)
    own = lax.all_gather(arrived, "x", axis=0, tiled=True)
    other = lax.ppermute(own, "c", [(0, 1), (1, 0)])

    ends = jnp.cumsum(image_lengths, dtype=jnp.int32)
    starts = ends - image_lengths
    first = block_index * block
    positions = first + jnp.arange(block, dtype=jnp.int32)
    seg = segment_of(positions, ends)
    onehot = seg[:, None] == jnp.arange(images, dtype=jnp.int32)[None, :]
    start_row = jnp.sum(jnp.where(onehot, starts[None, :], 0), axis=1, dtype=jnp.int32)
    seed_row = jnp.sum(jnp.where(onehot, probe_seeds[None, :], 0), axis=1, dtype=jnp.int32)
    signs = probe_signs(seed_row, positions - start_row, width).astype(bf16)
    kpos = first - SPAN * rows + jnp.arange(block + 2 * SPAN * rows, dtype=jnp.int32)
    valid = (kpos >= 0) & (kpos < block * n_block)
    segk = jnp.where(valid, segment_of(kpos, ends), -1)

    hh = pl.pallas_call(
        norm_kernel,
        out_shape=jax.ShapeDtypeStruct((2 * block, width), bf16),
        in_specs=[SMEM] + [VMEM] * 4,
        out_specs=VMEM,
        scratch_shapes=[pltpu.VMEM((rows, width), f32)],
        compiler_params=params(24),
    )(core_word, own, other, signs, in_gain[None, :])

    kv, q_early = pl.pallas_call(
        kv_kernel,
        out_shape=(
            jax.ShapeDtypeStruct((block, 4 * HEAD_DIM), bf16),
            jax.ShapeDtypeStruct((2 * block, LANES), bf16),
        ),
        in_specs=[VMEM, ANY],
        out_specs=(VMEM, VMEM),
        scratch_shapes=[pltpu.VMEM((width, 2 * LANES), bf16), pltpu.SemaphoreType.DMA],
        compiler_params=params(24),
        cost_estimate=pl.CostEstimate(flops=4 * block * width * 2 * LANES, bytes_accessed=4_000_000, transcendentals=0),
    )(hh, weights)
    neighbours = (moved(kv[rows:], 2), moved(kv, 1), kv, moved(kv, -1), moved(kv[:rows], -2))
    q, u = pl.pallas_call(
        q_kernel,
        out_shape=(
            jax.ShapeDtypeStruct((2 * block, q_width), bf16),
            jax.ShapeDtypeStruct((block, 3 * LANES), f32),
        ),
        in_specs=[VMEM, VMEM, VMEM, ANY],
        out_specs=(VMEM, VMEM),
        scratch_shapes=[pltpu.VMEM((width, 4 * LANES), bf16), pltpu.SemaphoreType.DMA],
        compiler_params=params(24),
        cost_estimate=pl.CostEstimate(flops=6 * block * width * 3 * LANES, bytes_accessed=6_000_000, transcendentals=0),
    )(hh, signs, q_early, weights)

    mine, theirs, share = pl.pallas_call(
        functools.partial(attend_kernel, rows),
        out_shape=(
            jax.ShapeDtypeStruct((rows, width), f32),
            jax.ShapeDtypeStruct((rows + 16, width), bf16),
            jax.ShapeDtypeStruct((1, images), f32),
        ),
        in_specs=[SMEM] + [VMEM] * 9 + [ANY],
        out_specs=(VMEM, VMEM, VMEM),
        scratch_shapes=[
            pltpu.VMEM((8 * rows, 4 * HEAD_DIM), bf16),
            pltpu.VMEM((width, 3 * LANES), bf16),
            pltpu.VMEM((block, 3 * LANES), bf16),
            pltpu.SemaphoreType.DMA,
        ],
        compiler_params=params(40),
        cost_estimate=pl.CostEstimate(flops=2_000_000_000, bytes_accessed=5_000_000, transcendentals=700_000),
    )(core_word, q, *neighbours, seg[:, None], segk[None, :], u, weights)

    theirs = lax.ppermute(theirs, "c", [(0, 1), (1, 0)])
    group = pl.pallas_call(
        join_kernel,
        out_shape=jax.ShapeDtypeStruct((n_x, rows + 16, quarter), bf16),
        in_specs=[VMEM] * 3,
        out_specs=VMEM,
        compiler_params=params(16),
    )(mine, share, theirs)
    groups = lax.all_to_all(group, "x", split_axis=0, concat_axis=0, tiled=True)
    velocity = jnp.sum(groups[:, :rows].astype(f32), axis=0).astype(bf16)
    share = jnp.sum(groups[:, rows:, :images].astype(f32), axis=(0, 1))
    divergence = jnp.sum(spread(share, COLUMN), axis=0) / width
    return (velocity, divergence)


def solution(mesh):
    n_seq, n_x = mesh.devices.shape
    n_y = 1
    while n_y * n_y * 2 < n_seq:
        n_y *= 2
    devices = mesh.devices.reshape(n_y, n_seq // 2 // n_y, 2, n_x)
    split = Mesh(devices, ("y", "z", "c", "x"))
    in_specs = (
        P(SEQ, None),
        P(SEQ, None),
        P(),
        P(),
        P(),
        P(SEQ, "x"),
        P(SEQ, None, "x"),
        P("x", SEQ),
    )
    out_specs = (P(SEQ, "x"), P())
    return jax.shard_map(body, mesh=split, in_specs=in_specs, out_specs=out_specs, check_vma=False)
```

```python
import functools

import jax
import jax.numpy as jnp
from jax import lax
from jax.experimental import pallas as pl
from jax.experimental.pallas import tpu as pltpu
from jax.sharding import Mesh
from jax.sharding import PartitionSpec as P

HEADS = 24
KV_HEADS = 8
HEAD_DIM = 96
GROUP = HEADS // KV_HEADS
SPAN = 3
SEQ = ("y", "z", "c")
COLUMN = ("y", "z")


def segment_of(pos, ends):
    return jnp.sum((ends[None, :] <= pos[:, None]).astype(jnp.int32), axis=1, dtype=jnp.int32)


def probe_signs(seed_row, local_row, width):
    columns = jnp.arange(width, dtype=jnp.int32)
    mixed = seed_row[:, None] * 40503 + local_row[:, None] * 69069 + columns[None, :] * 2654435
    mixed = mixed ^ jnp.right_shift(mixed, 15)
    mixed = mixed * 1597334677
    mixed = mixed ^ jnp.right_shift(mixed, 13)
    mixed = mixed * 668265263
    bit = jnp.right_shift(mixed, 11) & 1
    return (1 - 2 * bit).astype(jnp.float32)


def spread(array, axes):
    count = lax.axis_size(axes)
    copies = jnp.broadcast_to(array[None], (count,) + array.shape)
    return lax.all_to_all(copies, axes, split_axis=0, concat_axis=0, tiled=True)


def moved(array, by):
    count = lax.axis_size(COLUMN)
    pairs = [(i, i + by) for i in range(count) if 0 <= i + by < count]
    return lax.ppermute(array, COLUMN, pairs)


NT = (((1,), (1,)), ((), ()))
VMEM = pl.BlockSpec(memory_space=pltpu.VMEM)
SMEM = pl.BlockSpec(memory_space=pltpu.SMEM)
ANY = pl.BlockSpec(memory_space=pl.ANY)
LANES = 128


def params(mib):
    return pltpu.CompilerParams(vmem_limit_bytes=mib * 1024 * 1024)


def pack_kernel(depth, in_ref, out_ref, wide, tall):
    q_width = GROUP * HEAD_DIM
    tiles = wide.shape[1] // LANES
    k_first = 2 * q_width
    v_first = k_first + 2 * HEAD_DIM
    o_first = v_first + 2 * HEAD_DIM
    held = in_ref[...].astype(jnp.float32)
    tall[...] = jnp.zeros_like(tall)
    for core in range(2):
        k, q = core * HEAD_DIM, core * q_width
        wide[:, :HEAD_DIM] = held[:, k_first + k : k_first + k + HEAD_DIM]
        wide[:, HEAD_DIM : 2 * HEAD_DIM] = held[:, v_first + k : v_first + k + HEAD_DIM]
        wide[:, 2 * HEAD_DIM : 2 * HEAD_DIM + q_width] = held[:, q : q + q_width]
        wide[:, 2 * HEAD_DIM + q_width :] = held[:, o_first + q : o_first + q + q_width]
        for tile in range(tiles):
            tall[tile * depth : (tile + 1) * depth, :] = wide[:, tile * LANES : (tile + 1) * LANES]
        piece = tall[...].astype(jnp.bfloat16)
        for z in range(out_ref.shape[0] // 2):
            out_ref[2 * z + core] = piece


def unpack_kernel(depth, in_ref, out_ref, tall, wide):
    for source in range(in_ref.shape[0]):
        tall[...] = in_ref[source].astype(jnp.float32)
        for tile in range(out_ref.shape[1] // LANES):
            wide[source * depth : (source + 1) * depth, tile * LANES : (tile + 1) * LANES] = tall[
                tile * depth : (tile + 1) * depth, :
            ]
    out_ref[...] = wide[...].astype(jnp.bfloat16)


def norm_kernel(core_ref, own_ref, other_ref, signs_ref, gain_ref, out_ref, wide):
    rows, width = wide.shape
    members = own_ref.shape[0] // rows
    quarter = width // members
    gain = gain_ref[...]
    for half in range(2):
        mine = core_ref[0] == half
        for x in range(members):
            a, b = x * rows, (x + 1) * rows
            both = jnp.where(mine, own_ref[a:b, :].astype(jnp.float32), other_ref[a:b, :].astype(jnp.float32))
            wide[:, x * quarter : (x + 1) * quarter] = both[:, :quarter]
        x = wide[...]
        signs = signs_ref[half * rows : (half + 1) * rows, :].astype(jnp.float32)
        inv = lax.rsqrt(jnp.sum(x * x, axis=1, keepdims=True) / width + 1e-06)
        along = jnp.sum(x * signs, axis=1, keepdims=True) / width
        out_ref[half * rows : (half + 1) * rows, :] = (x * inv * gain).astype(jnp.bfloat16)
        out_ref[(2 + half) * rows : (3 + half) * rows, :] = (
            (signs * inv - x * (inv * inv * inv * along)) * gain
        ).astype(jnp.bfloat16)


def project_kernel(hh_any, signs_any, w_any, kv_ref, head_ref, tail_ref, q_ref, u_ref, hh, signs, weight, sems):
    block = kv_ref.shape[0]
    rows = block // 2
    both = 2 * HEAD_DIM
    q_width = q_ref.shape[1]
    depth = weight.shape[1]
    thirds = weight.shape[0]
    fetches = []
    for k in range(thirds):
        at = pl.ds(k * depth, depth)
        fetches.append(
            (
                pltpu.make_async_copy(w_any.at[at, :], weight.at[k], sems.at[k, 0]),
                pltpu.make_async_copy(hh_any.at[:, at], hh.at[k], sems.at[k, 1]),
                pltpu.make_async_copy(signs_any.at[:, at], signs.at[k], sems.at[k, 2]),
            )
        )
        for fetch in fetches[k]:
            fetch.start()
    for k in range(thirds):
        for fetch in fetches[k]:
            fetch.wait()
        r_k = jnp.dot(hh[k], weight[k, :, : 4 * LANES], preferred_element_type=jnp.float32)
        u_k = jnp.dot(signs[k], weight[k, :, 3 * LANES :], preferred_element_type=jnp.float32)
        r, u = (r_k, u_k) if k == 0 else (r + r_k, u + u_k)
    for part in range(2):
        a, b = part * block, (part + 1) * block
        made = r[a:b, :both].astype(jnp.bfloat16)
        kv_ref[:, part * both : (part + 1) * both] = made
        head_ref[:, part * both : (part + 1) * both] = made[:rows]
        tail_ref[:, part * both : (part + 1) * both] = made[rows:]
        q_ref[a:b, :] = r[a:b, both : both + q_width].astype(jnp.bfloat16)
    u_ref[...] = u


def attend_kernel(
    rows, core_ref, q_ref, far_before, before, here, after, far_after, segq_ref, segk_ref, u_ref, w_any,
    mine_ref, theirs_ref, share_ref, window, o_ext, weight, w_sem,
):
    block = 2 * rows
    reach = (2 * SPAN + 1) * rows
    q_width = GROUP * HEAD_DIM
    o_width = weight.shape[1]
    fetch = pltpu.make_async_copy(w_any.at[:, pl.ds(w_any.shape[1] - o_width, o_width)], weight, w_sem)
    fetch.start()
    shift = o_width - q_width
    window[0:rows] = far_before[...]
    window[rows : rows + block] = before[...]
    window[rows + block : rows + 2 * block] = here[...]
    window[rows + 2 * block : rows + 3 * block] = after[...]
    window[rows + 3 * block : 2 * rows + 3 * block] = far_after[...]
    scale = 1.0 / HEAD_DIM**0.5
    to_exp2 = scale * 1.4426950408889634
    o_ext[:, :shift] = jnp.zeros((block, shift), jnp.bfloat16)
    images = share_ref.shape[1]
    share = jnp.zeros((1, images), jnp.float32)
    for tile in range(2):
        lo = tile * rows
        keys = window[lo : lo + reach, 0:HEAD_DIM]
        values = window[lo : lo + reach, HEAD_DIM : 2 * HEAD_DIM]
        keys_t = window[lo : lo + reach, 2 * HEAD_DIM : 3 * HEAD_DIM]
        values_t = window[lo : lo + reach, 3 * HEAD_DIM : 4 * HEAD_DIM]
        mask = segq_ref[lo : lo + rows, :] == segk_ref[:, lo : lo + reach]
        terms = jnp.zeros((rows, 1), jnp.float32)
        for head in range(GROUP):
            a, b = head * HEAD_DIM, (head + 1) * HEAD_DIM
            q = q_ref[lo : lo + rows, a:b]
            q_t = q_ref[block + lo : block + lo + rows, a:b]
            s = lax.dot_general(q, keys, NT, preferred_element_type=jnp.float32)
            s_t = lax.dot_general(q_t, keys, NT, preferred_element_type=jnp.float32)
            s_t += lax.dot_general(q, keys_t, NT, preferred_element_type=jnp.float32)
            s = jnp.where(mask, s, -1e30)
            e = jnp.exp2((s - jnp.max(s, axis=1, keepdims=True)) * to_exp2)
            inv = 1.0 / jnp.sum(e, axis=1, keepdims=True)
            mean = jnp.sum(e * s_t, axis=1, keepdims=True) * inv
            e_t = (e * ((s_t - mean) * scale)).astype(jnp.bfloat16)
            e = e.astype(jnp.bfloat16)
            out = jnp.dot(e, values, preferred_element_type=jnp.float32) * inv
            out_t = jnp.dot(e_t, values, preferred_element_type=jnp.float32)
            out_t += jnp.dot(e, values_t, preferred_element_type=jnp.float32)
            out_t = (out_t * inv).astype(jnp.bfloat16).astype(jnp.float32)
            o_ext[lo : lo + rows, shift + a : shift + b] = out.astype(jnp.bfloat16)
            terms += jnp.sum(out_t * u_ref[lo : lo + rows, shift + a : shift + b], axis=1, keepdims=True)
        numbers = lax.broadcasted_iota(jnp.int32, (rows, images), 1)
        hit = segq_ref[lo : lo + rows, :] == numbers
        share += jnp.sum(jnp.where(hit, terms, 0.0), axis=0, keepdims=True)
    share_ref[...] = share
    core = core_ref[0]
    own = o_ext[pl.ds(pl.multiple_of(core * rows, rows), rows), :]
    other = o_ext[pl.ds(pl.multiple_of((1 - core) * rows, rows), rows), :]
    both = jnp.concatenate([other, own], axis=0)
    fetch.wait()
    step = weight.shape[0] // 4
    for part in range(4):
        a, b = part * step, (part + 1) * step
        r = lax.dot_general(weight[a:b, :], both, NT, preferred_element_type=jnp.float32)
        theirs_ref[a:b, :] = r[:, :rows].astype(jnp.bfloat16)
        mine_ref[a:b, :] = r[:, rows:]


def body(owned_rows, arrival, image_lengths, probe_seeds, in_gain, w_q, w_kv, w_out):
    bf16, f32 = jnp.bfloat16, jnp.float32
    rows, width = owned_rows.shape
    n_x, n_z, n_seq = lax.axis_size("x"), lax.axis_size("z"), lax.axis_size(SEQ)
    core, member = lax.axis_index("c"), lax.axis_index("x")
    core_word = jnp.reshape(core, (1,)).astype(jnp.int32)
    n_block = lax.axis_size(COLUMN)
    block_index = lax.axis_index(COLUMN)
    quarter = width // n_x
    depth = w_q.shape[0]
    block = 2 * rows
    images = image_lengths.shape[0]
    q_width = GROUP * HEAD_DIM
    columns = 2 * HEAD_DIM + 2 * q_width

    tall_rows = -(-depth * (columns // LANES) // 16) * 16
    pieces = pl.pallas_call(
        functools.partial(pack_kernel, depth),
        out_shape=jax.ShapeDtypeStruct((2 * n_z, tall_rows, LANES), bf16),
        in_specs=[VMEM],
        out_specs=VMEM,
        scratch_shapes=[pltpu.VMEM((depth, columns), f32), pltpu.VMEM((tall_rows, LANES), f32)],
        compiler_params=params(50),
    )(jnp.concatenate([w_q, w_kv[:, 0], w_kv[:, 1], w_out.T], axis=1))
    strip = lax.all_to_all(pieces, ("z", "c"), split_axis=0, concat_axis=0, tiled=True)
    strip = pl.pallas_call(
        functools.partial(unpack_kernel, depth),
        out_shape=jax.ShapeDtypeStruct((2 * n_z * depth, columns), bf16),
        in_specs=[VMEM],
        out_specs=VMEM,
        scratch_shapes=[pltpu.VMEM((tall_rows, LANES), f32), pltpu.VMEM((2 * n_z * depth, columns), f32)],
        compiler_params=params(50),
    )(strip)
    weights = lax.all_gather(strip, "y", axis=0, tiled=True)

    part = lax.dynamic_slice_in_dim(owned_rows, member * quarter, quarter, 1)
    padded = -(-quarter // LANES) * LANES
    part = jnp.pad(part, ((0, 0), (0, padded - quarter))).reshape(rows, 1, padded)
    part, strip = lax.optimization_barrier((part, strip))
    arrived = lax.all_to_all(part, SEQ, split_axis=0, concat_axis=0, tiled=True)
    arrived = jnp.take(arrived.reshape(rows, padded), arrival[0], axis=0, mode="clip")
    own = lax.all_gather(arrived, "x", axis=0, tiled=True)
    other = lax.ppermute(own, "c", [(0, 1), (1, 0)])

    ends = jnp.cumsum(image_lengths, dtype=jnp.int32)
    starts = ends - image_lengths
    first = block_index * block
    positions = first + jnp.arange(block, dtype=jnp.int32)
    seg = segment_of(positions, ends)
    onehot = seg[:, None] == jnp.arange(images, dtype=jnp.int32)[None, :]
    start_row = jnp.sum(jnp.where(onehot, starts[None, :], 0), axis=1, dtype=jnp.int32)
    seed_row = jnp.sum(jnp.where(onehot, probe_seeds[None, :], 0), axis=1, dtype=jnp.int32)
    signs = probe_signs(seed_row, positions - start_row, width).astype(bf16)
    kpos = first - SPAN * rows + jnp.arange(block + 2 * SPAN * rows, dtype=jnp.int32)
    valid = (kpos >= 0) & (kpos < block * n_block)
    segk = jnp.where(valid, segment_of(kpos, ends), -1)

    hh = pl.pallas_call(
        norm_kernel,
        out_shape=jax.ShapeDtypeStruct((2 * block, width), bf16),
        in_specs=[SMEM] + [VMEM] * 4,
        out_specs=VMEM,
        scratch_shapes=[pltpu.VMEM((rows, width), f32)],
        compiler_params=params(50),
    )(core_word, own, other, signs, in_gain[None, :])

    kv, head, tail, q, u = pl.pallas_call(
        project_kernel,
        out_shape=(
            jax.ShapeDtypeStruct((block, 4 * HEAD_DIM), bf16),
            jax.ShapeDtypeStruct((rows, 4 * HEAD_DIM), bf16),
            jax.ShapeDtypeStruct((rows, 4 * HEAD_DIM), bf16),
            jax.ShapeDtypeStruct((2 * block, q_width), bf16),
            jax.ShapeDtypeStruct((block, 3 * LANES), f32),
        ),
        in_specs=[ANY] * 3,
        out_specs=(VMEM,) * 5,
        scratch_shapes=[
            pltpu.VMEM((3, 2 * block, width // 3), bf16),
            pltpu.VMEM((3, block, width // 3), bf16),
            pltpu.VMEM((3, width // 3, columns), bf16),
            pltpu.SemaphoreType.DMA((3, 3)),
        ],
        compiler_params=params(50),
        cost_estimate=pl.CostEstimate(flops=6 * block * width * columns, bytes_accessed=8_000_000, transcendentals=0),
    )(hh, signs, weights)
    neighbours = (moved(tail, 2), moved(kv, 1), kv, moved(kv, -1), moved(head, -2))

    mine, theirs, share = pl.pallas_call(
        functools.partial(attend_kernel, rows),
        out_shape=(
            jax.ShapeDtypeStruct((width, rows), f32),
            jax.ShapeDtypeStruct((width, rows), bf16),
            jax.ShapeDtypeStruct((1, images), f32),
        ),
        in_specs=[SMEM] + [VMEM] * 9 + [ANY],
        out_specs=(VMEM, VMEM, VMEM),
        scratch_shapes=[
            pltpu.VMEM((8 * rows, 4 * HEAD_DIM), bf16),
            pltpu.VMEM((block, 3 * LANES), bf16),
            pltpu.VMEM((width, 3 * LANES), bf16),
            pltpu.SemaphoreType.DMA,
        ],
        compiler_params=params(50),
        cost_estimate=pl.CostEstimate(flops=2_000_000_000, bytes_accessed=5_000_000, transcendentals=700_000),
    )(core_word, q, *neighbours, seg[:, None], segk[None, :], u, weights)

    theirs = lax.ppermute(theirs, "c", [(0, 1), (1, 0)])
    group = (mine + theirs.astype(f32)).astype(bf16)
    velocity = lax.psum_scatter(group, "x", scatter_dimension=0, tiled=True).T
    share, group = lax.optimization_barrier((share, group))
    share = jnp.sum(spread(share[0], ("y", "c")), axis=0)
    divergence = jnp.sum(spread(share, ("z", "x")), axis=0) / width
    return (velocity, divergence)


def solution(mesh):
    n_seq, n_x = mesh.devices.shape
    n_y = 1
    while n_y * n_y * 2 < n_seq:
        n_y *= 2
    devices = mesh.devices.reshape(n_y, n_seq // 2 // n_y, 2, n_x)
    split = Mesh(devices, ("y", "z", "c", "x"))
    in_specs = (
        P(SEQ, None),
        P(SEQ, None),
        P(),
        P(),
        P(),
        P(SEQ, "x"),
        P(SEQ, None, "x"),
        P("x", SEQ),
    )
    out_specs = (P(SEQ, "x"), P())
    return jax.shard_map(body, mesh=split, in_specs=in_specs, out_specs=out_specs, check_vma=False)
```

```python
import functools

import jax
import jax.numpy as jnp
from jax import lax
from jax.experimental import pallas as pl
from jax.experimental.pallas import tpu as pltpu
from jax.sharding import Mesh
from jax.sharding import PartitionSpec as P

HEADS = 24
KV_HEADS = 8
HEAD_DIM = 96
GROUP = HEADS // KV_HEADS
SPAN = 3
SEQ = ("y", "z", "c")
COLUMN = ("y", "z")


def segment_of(pos, ends):
    return jnp.sum((ends[None, :] <= pos[:, None]).astype(jnp.int32), axis=1, dtype=jnp.int32)


def probe_signs(seed_row, local_row, columns):
    mixed = seed_row[:, None] * 40503 + local_row[:, None] * 69069 + columns[None, :] * 2654435
    mixed = mixed ^ jnp.right_shift(mixed, 15)
    mixed = mixed * 1597334677
    mixed = mixed ^ jnp.right_shift(mixed, 13)
    mixed = mixed * 668265263
    bit = jnp.right_shift(mixed, 11) & 1
    return (1 - 2 * bit).astype(jnp.float32)


def spread(array, axes):
    count = lax.axis_size(axes)
    copies = jnp.broadcast_to(array[None], (count,) + array.shape)
    return lax.all_to_all(copies, axes, split_axis=0, concat_axis=0, tiled=True)


def moved(array, by):
    count = lax.axis_size(COLUMN)
    pairs = [(i, i + by) for i in range(count) if 0 <= i + by < count]
    return lax.ppermute(array, COLUMN, pairs)


NT = (((1,), (1,)), ((), ()))
VMEM = pl.BlockSpec(memory_space=pltpu.VMEM)
SMEM = pl.BlockSpec(memory_space=pltpu.SMEM)
ANY = pl.BlockSpec(memory_space=pl.ANY)
LANES = 128


def params(mib):
    return pltpu.CompilerParams(vmem_limit_bytes=mib * 1024 * 1024)


def pack_kernel(depth, core_ref, in_ref, own_ref, other_ref, wide, tall):
    q_width = GROUP * HEAD_DIM
    tiles = wide.shape[1] // LANES
    k_first = 2 * q_width
    v_first = k_first + 2 * HEAD_DIM
    o_first = v_first + 2 * HEAD_DIM
    held = in_ref[...].astype(jnp.float32)
    tall[...] = jnp.zeros_like(tall)
    for core in range(2):
        k, q = core * HEAD_DIM, core * q_width
        wide[:, :HEAD_DIM] = held[:, k_first + k : k_first + k + HEAD_DIM]
        wide[:, HEAD_DIM : 2 * HEAD_DIM] = held[:, v_first + k : v_first + k + HEAD_DIM]
        wide[:, 2 * HEAD_DIM : 2 * HEAD_DIM + q_width] = held[:, q : q + q_width]
        wide[:, 2 * HEAD_DIM + q_width :] = held[:, o_first + q : o_first + q + q_width]
        for tile in range(tiles):
            tall[tile * depth : (tile + 1) * depth, :] = wide[:, tile * LANES : (tile + 1) * LANES]
        piece = tall[...].astype(jnp.bfloat16)

        @pl.when(core_ref[0] == core)
        def _(piece=piece):
            own_ref[...] = piece

        @pl.when(core_ref[0] != core)
        def _(piece=piece):
            other_ref[...] = piece


def copies_kernel(core_ref, own_ref, other_ref, out_ref):
    @pl.when(core_ref[0] == 0)
    def _():
        for to in range(out_ref.shape[0]):
            out_ref[to, 0] = own_ref[...]
            out_ref[to, 1] = other_ref[...]

    @pl.when(core_ref[0] != 0)
    def _():
        for to in range(out_ref.shape[0]):
            out_ref[to, 0] = other_ref[...]
            out_ref[to, 1] = own_ref[...]


def unpack_kernel(depth, in_ref, out_ref, tall, wide):
    for source in range(in_ref.shape[0]):
        tall[...] = in_ref[source].astype(jnp.float32)
        for tile in range(out_ref.shape[1] // LANES):
            wide[source * depth : (source + 1) * depth, tile * LANES : (tile + 1) * LANES] = tall[
                tile * depth : (tile + 1) * depth, :
            ]
    out_ref[...] = wide[...].astype(jnp.bfloat16)


def project_kernel(
    side, unit, core_ref, own_ref, other_ref, signs_ref, gain_ref, w_any,
    kv_ref, qu_ref, wide, hh, weight, sem,
):
    rows, width = wide.shape
    block = 2 * rows
    members = own_ref.shape[0] // rows
    quarter = width // members
    fetch = pltpu.make_async_copy(w_any, weight, sem)
    fetch.start()
    gain = gain_ref[...]
    for half in range(2):
        mine = core_ref[0] == half
        for x in range(members):
            a, b = x * rows, (x + 1) * rows
            held = jnp.where(mine, own_ref[a:b, :].astype(jnp.float32), other_ref[a:b, :].astype(jnp.float32))

            @pl.when(core_ref[0] == 0)
            def _(x=x, held=held):
                wide[:, x * quarter : (x + 1) * quarter] = held[:, :quarter]

            @pl.when(core_ref[0] != 0)
            def _(x=x, held=held):
                for i in range(quarter // unit):
                    y, z = divmod(x * quarter // unit + i, side)
                    to = (z * side + y) * unit
                    wide[:, to : to + unit] = held[:, i * unit : (i + 1) * unit]

        x = wide[...]
        signs = signs_ref[half * rows : (half + 1) * rows, :].astype(jnp.float32)
        inv = lax.rsqrt(jnp.sum(x * x, axis=1, keepdims=True) / width + 1e-06)
        along = jnp.sum(x * signs, axis=1, keepdims=True) / width
        hh[half * rows : (half + 1) * rows, :] = (x * inv * gain).astype(jnp.bfloat16)
        hh[(2 + half) * rows : (3 + half) * rows, :] = (
            (signs * inv - x * (inv * inv * inv * along)) * gain
        ).astype(jnp.bfloat16)
    fetch.wait()
    both = 2 * HEAD_DIM
    q_width = GROUP * HEAD_DIM
    for part in range(2):
        a, b = part * block, (part + 1) * block
        r = jnp.dot(hh[a:b, :], weight[:, : 4 * LANES], preferred_element_type=jnp.float32)
        at = part * HEAD_DIM
        kv_ref[:, at : at + HEAD_DIM] = r[:, :HEAD_DIM].astype(jnp.bfloat16)
        kv_ref[:, both + at : both + at + HEAD_DIM] = r[:, HEAD_DIM:both].astype(jnp.bfloat16)
        qu_ref[a:b, :q_width] = r[:, both : both + q_width].astype(jnp.bfloat16)
    u = jnp.dot(signs_ref[...], weight[:, 3 * LANES :], preferred_element_type=jnp.float32)
    qu_ref[2 * block :, :] = u.astype(jnp.bfloat16)


def attend_kernel(
    rows, side, core_ref, qu_ref, far_before, before, here, after, far_after, segq_ref, segk_ref, w_any,
    mine_ref, theirs_ref, share_ref, window, o_ext, weight, flat, w_sem,
):
    block = 2 * rows
    reach = (2 * SPAN + 1) * rows
    q_width = GROUP * HEAD_DIM
    o_width = weight.shape[1]
    fetch = pltpu.make_async_copy(w_any.at[:, pl.ds(w_any.shape[1] - o_width, o_width)], weight, w_sem)
    fetch.start()
    shift = o_width - q_width
    window[0:rows] = far_before[...]
    window[rows : rows + block] = before[...]
    window[rows + block : rows + 2 * block] = here[...]
    window[rows + 2 * block : rows + 3 * block] = after[...]
    window[rows + 3 * block : 2 * rows + 3 * block] = far_after[...]
    scale = 1.0 / HEAD_DIM**0.5
    to_exp2 = scale * 1.4426950408889634
    o_ext[:, :shift] = jnp.zeros((block, shift), jnp.bfloat16)
    images = share_ref.shape[1]
    share = jnp.zeros((1, images), jnp.float32)
    both = 2 * HEAD_DIM
    for tile in range(2):
        lo = tile * rows
        keys = window[lo : lo + reach, :both]
        values = window[lo : lo + reach, both:]

        def heads(first):
            parts = [
                qu_ref[first + lo : first + lo + rows, h * HEAD_DIM : (h + 1) * HEAD_DIM] for h in range(GROUP)
            ]
            return jnp.concatenate(parts, axis=0)

        q, q_t = heads(0), heads(block)
        segq = segq_ref[lo : lo + rows, :]
        mask = jnp.concatenate([segq] * GROUP, axis=0) == segk_ref[:, lo : lo + reach]
        s = lax.dot_general(q, keys[:, :HEAD_DIM], NT, preferred_element_type=jnp.float32)
        s_t = lax.dot_general(
            jnp.concatenate([q_t, q], axis=1), keys, NT, preferred_element_type=jnp.float32
        )
        s = jnp.where(mask, s, -1e30)
        e = jnp.exp2((s - jnp.max(s, axis=1, keepdims=True)) * to_exp2)
        inv = 1.0 / jnp.sum(e, axis=1, keepdims=True)
        mean = jnp.sum(e * s_t, axis=1, keepdims=True) * inv
        e_t = (e * ((s_t - mean) * scale)).astype(jnp.bfloat16)
        e = e.astype(jnp.bfloat16)
        made = jnp.dot(e, values, preferred_element_type=jnp.float32)
        out = (made[:, :HEAD_DIM] * inv).astype(jnp.bfloat16)
        out_t = jnp.dot(e_t, values[:, :HEAD_DIM], preferred_element_type=jnp.float32) + made[:, HEAD_DIM:]
        out_t = (out_t * inv).astype(jnp.bfloat16).astype(jnp.float32)
        terms = jnp.zeros((rows, 1), jnp.float32)
        for head in range(GROUP):
            a, b = shift + head * HEAD_DIM, shift + (head + 1) * HEAD_DIM
            at = head * rows
            u = qu_ref[2 * block + lo : 2 * block + lo + rows, a:b].astype(jnp.float32)
            o_ext[lo : lo + rows, a:b] = out[at : at + rows]
            terms += jnp.sum(out_t[at : at + rows] * u, axis=1, keepdims=True)
        numbers = lax.broadcasted_iota(jnp.int32, (rows, images), 1)
        share += jnp.sum(jnp.where(segq == numbers, terms, 0.0), axis=0, keepdims=True)
    share_ref[...] = share
    core = core_ref[0]
    own = o_ext[pl.ds(pl.multiple_of(core * rows, rows), rows), :]
    other = o_ext[pl.ds(pl.multiple_of((1 - core) * rows, rows), rows), :]
    both = jnp.concatenate([other, own], axis=0)
    fetch.wait()
    width = weight.shape[0]
    step, unit = width // 4, width // side**2
    for part in range(4):
        a, b = part * step, (part + 1) * step
        r = lax.dot_general(weight[a:b, :], both, NT, preferred_element_type=jnp.float32)

        @pl.when(core == 0)
        def _(a=a, b=b, r=r):
            theirs_ref[a:b, :] = r[:, :rows].astype(jnp.bfloat16)
            mine_ref[a:b, :] = r[:, rows:]

        @pl.when(core != 0)
        def _(a=a, r=r):
            for i in range(step // unit):
                z, y = divmod(a // unit + i, side)
                to = (y * side + z) * unit
                flat[to : to + unit, :] = r[i * unit : (i + 1) * unit, :rows]
                mine_ref[to : to + unit, :] = r[i * unit : (i + 1) * unit, rows:]

    @pl.when(core != 0)
    def _():
        theirs_ref[...] = flat[...].astype(jnp.bfloat16)


def body(owned_rows, arrival, image_lengths, probe_seeds, in_gain, w_q, w_kv, w_out):
    bf16, f32 = jnp.bfloat16, jnp.float32
    rows, width = owned_rows.shape
    n_x, n_z, n_seq = lax.axis_size("x"), lax.axis_size("z"), lax.axis_size(SEQ)
    core, member = lax.axis_index("c"), lax.axis_index("x")
    core_word = jnp.reshape(core, (1,)).astype(jnp.int32)
    n_block = lax.axis_size(COLUMN)
    block_index = lax.axis_index(COLUMN)
    quarter = width // n_x
    depth = w_q.shape[0]
    block = 2 * rows
    images = image_lengths.shape[0]
    q_width = GROUP * HEAD_DIM
    columns = 2 * HEAD_DIM + 2 * q_width

    tall_rows = -(-depth * (columns // LANES) // 16) * 16
    piece = jax.ShapeDtypeStruct((tall_rows, LANES), bf16)
    own_piece, other_piece = pl.pallas_call(
        functools.partial(pack_kernel, depth),
        out_shape=(piece, piece),
        in_specs=[SMEM, VMEM],
        out_specs=(VMEM, VMEM),
        scratch_shapes=[pltpu.VMEM((depth, columns), f32), pltpu.VMEM((tall_rows, LANES), f32)],
        compiler_params=params(50),
    )(core_word, jnp.concatenate([w_q, w_kv[:, 0], w_kv[:, 1], w_out.T], axis=1))
    other_piece = lax.ppermute(other_piece, "c", [(0, 1), (1, 0)])
    pieces = pl.pallas_call(
        copies_kernel,
        out_shape=jax.ShapeDtypeStruct((n_z, 2, tall_rows, LANES), bf16),
        in_specs=[SMEM] + [VMEM] * 2,
        out_specs=VMEM,
        compiler_params=params(50),
    )(core_word, own_piece, other_piece)
    side = range(n_z)
    place = lambda y, z, c: (y * n_z + z) * 2 + c
    by_z = [[place(y, z, 0) for z in side] for y in side] + [[place(y, z, 1) for y in side] for z in side]
    by_y = [[place(y, z, 0) for y in side] for z in side] + [[place(y, z, 1) for z in side] for y in side]
    strip = lax.all_to_all(pieces, SEQ, split_axis=0, concat_axis=0, tiled=True, axis_index_groups=by_z)
    strip = strip.reshape(2 * n_z, tall_rows, LANES)
    strip = pl.pallas_call(
        functools.partial(unpack_kernel, depth),
        out_shape=jax.ShapeDtypeStruct((2 * n_z * depth, columns), bf16),
        in_specs=[VMEM],
        out_specs=VMEM,
        scratch_shapes=[pltpu.VMEM((tall_rows, LANES), f32), pltpu.VMEM((2 * n_z * depth, columns), f32)],
        compiler_params=params(50),
    )(strip)
    weights = lax.all_gather(strip, SEQ, axis=0, tiled=True, axis_index_groups=by_y)

    part = lax.dynamic_slice_in_dim(owned_rows, member * quarter, quarter, 1)
    padded = -(-quarter // LANES) * LANES
    part = jnp.pad(part, ((0, 0), (0, padded - quarter))).reshape(rows, 2, padded // 2)
    part, strip = lax.optimization_barrier((part, strip))
    arrived = lax.all_to_all(part, SEQ, split_axis=0, concat_axis=0, tiled=True)
    arrived = jnp.take(arrived.reshape(rows, padded), arrival[0], axis=0, mode="clip")
    own = lax.all_gather(arrived, "x", axis=0, tiled=True)
    own, image_lengths, probe_seeds = lax.optimization_barrier((own, image_lengths, probe_seeds))
    other = lax.ppermute(own, "c", [(0, 1), (1, 0)])

    ends = jnp.cumsum(image_lengths, dtype=jnp.int32)
    starts = ends - image_lengths
    first = block_index * block
    positions = first + jnp.arange(block, dtype=jnp.int32)
    seg = segment_of(positions, ends)
    onehot = seg[:, None] == jnp.arange(images, dtype=jnp.int32)[None, :]
    start_row = jnp.sum(jnp.where(onehot, starts[None, :], 0), axis=1, dtype=jnp.int32)
    seed_row = jnp.sum(jnp.where(onehot, probe_seeds[None, :], 0), axis=1, dtype=jnp.int32)
    unit = 2 * depth
    turned = lambda row: jnp.transpose(row.reshape(n_z, n_z, unit), (1, 0, 2)).reshape(width)
    numbers = jnp.arange(width, dtype=jnp.int32)
    numbers = jnp.where(core == 0, numbers, turned(numbers))
    gain = jnp.where(core == 0, in_gain, turned(in_gain))
    signs = probe_signs(seed_row, positions - start_row, numbers).astype(bf16)
    kpos = first - SPAN * rows + jnp.arange(block + 2 * SPAN * rows, dtype=jnp.int32)
    valid = (kpos >= 0) & (kpos < block * n_block)
    segk = jnp.where(valid, segment_of(kpos, ends), -1)

    kv, qu = pl.pallas_call(
        functools.partial(project_kernel, n_z, unit),
        out_shape=(
            jax.ShapeDtypeStruct((block, 4 * HEAD_DIM), bf16),
            jax.ShapeDtypeStruct((3 * block, 3 * LANES), bf16),
        ),
        in_specs=[SMEM] + [VMEM] * 4 + [ANY],
        out_specs=(VMEM,) * 2,
        scratch_shapes=[
            pltpu.VMEM((rows, width), f32),
            pltpu.VMEM((2 * block, width), bf16),
            pltpu.VMEM((width, columns), bf16),
            pltpu.SemaphoreType.DMA,
        ],
        compiler_params=params(50),
        cost_estimate=pl.CostEstimate(flops=6 * block * width * columns, bytes_accessed=8_000_000, transcendentals=0),
    )(core_word, own, other, signs, gain[None, :], weights)
    neighbours = (moved(kv[rows:], 2), moved(kv, 1), kv, moved(kv, -1), moved(kv[:rows], -2))

    mine, theirs, share = pl.pallas_call(
        functools.partial(attend_kernel, rows, n_z),
        out_shape=(
            jax.ShapeDtypeStruct((width, rows), f32),
            jax.ShapeDtypeStruct((width, rows), bf16),
            jax.ShapeDtypeStruct((1, images), f32),
        ),
        in_specs=[SMEM] + [VMEM] * 8 + [ANY],
        out_specs=(VMEM, VMEM, VMEM),
        scratch_shapes=[
            pltpu.VMEM((8 * rows, 4 * HEAD_DIM), bf16),
            pltpu.VMEM((block, 3 * LANES), bf16),
            pltpu.VMEM((width, 3 * LANES), bf16),
            pltpu.VMEM((width, rows), f32),
            pltpu.SemaphoreType.DMA,
        ],
        compiler_params=params(50),
        cost_estimate=pl.CostEstimate(flops=2_000_000_000, bytes_accessed=5_000_000, transcendentals=700_000),
    )(core_word, qu, *neighbours, seg[:, None], segk[None, :], weights)

    theirs = lax.ppermute(theirs, "c", [(0, 1), (1, 0)])
    group = (mine + theirs.astype(f32)).astype(bf16)
    velocity = lax.psum_scatter(group, "x", scatter_dimension=0, tiled=True).T
    share, group = lax.optimization_barrier((share, group))
    share = jnp.sum(spread(share[0], ("y", "c")), axis=0)
    divergence = jnp.sum(spread(share, ("z", "x")), axis=0) / width
    return (velocity, divergence)


def solution(mesh):
    n_seq, n_x = mesh.devices.shape
    n_y = 1
    while n_y * n_y * 2 < n_seq:
        n_y *= 2
    devices = mesh.devices.reshape(n_y, n_seq // 2 // n_y, 2, n_x)
    split = Mesh(devices, ("y", "z", "c", "x"))
    in_specs = (
        P(SEQ, None),
        P(SEQ, None),
        P(),
        P(),
        P(),
        P(SEQ, "x"),
        P(SEQ, None, "x"),
        P("x", SEQ),
    )
    out_specs = (P(SEQ, "x"), P())
    return jax.shard_map(body, mesh=split, in_specs=in_specs, out_specs=out_specs, check_vma=False)
```

```python
import functools

import jax
import jax.numpy as jnp
from jax import lax
from jax.experimental import pallas as pl
from jax.experimental.pallas import tpu as pltpu
from jax.sharding import Mesh
from jax.sharding import PartitionSpec as P

HEADS = 24
KV_HEADS = 8
HEAD_DIM = 96
GROUP = HEADS // KV_HEADS
SPAN = 3
SEQ = ("y", "z", "c")
COLUMN = ("y", "z")


def segment_of(pos, ends):
    return jnp.sum((ends[None, :] <= pos[:, None]).astype(jnp.int32), axis=1, dtype=jnp.int32)


def probe_signs(seed_row, local_row, columns):
    mixed = seed_row[:, None] * 40503 + local_row[:, None] * 69069 + columns[None, :] * 2654435
    mixed = mixed ^ jnp.right_shift(mixed, 15)
    mixed = mixed * 1597334677
    mixed = mixed ^ jnp.right_shift(mixed, 13)
    mixed = mixed * 668265263
    bit = jnp.right_shift(mixed, 11) & 1
    return (1 - 2 * bit).astype(jnp.float32)


def spread(array, axes):
    count = lax.axis_size(axes)
    copies = jnp.broadcast_to(array[None], (count,) + array.shape)
    return lax.all_to_all(copies, axes, split_axis=0, concat_axis=0, tiled=True)


def moved(array, by):
    count = lax.axis_size(COLUMN)
    pairs = [(i, i + by) for i in range(count) if 0 <= i + by < count]
    return lax.ppermute(array, COLUMN, pairs)


NT = (((1,), (1,)), ((), ()))
VMEM = pl.BlockSpec(memory_space=pltpu.VMEM)
SMEM = pl.BlockSpec(memory_space=pltpu.SMEM)
ANY = pl.BlockSpec(memory_space=pl.ANY)
LANES = 128


def params(mib):
    return pltpu.CompilerParams(vmem_limit_bytes=mib * 1024 * 1024)


def pack_kernel(depth, core_ref, in_ref, own_ref, other_ref, wide, tall):
    q_width = GROUP * HEAD_DIM
    tiles = wide.shape[1] // LANES
    k_first = 2 * q_width
    v_first = k_first + 2 * HEAD_DIM
    o_first = v_first + 2 * HEAD_DIM
    held = in_ref[...].astype(jnp.float32)
    tall[...] = jnp.zeros_like(tall)
    for core in range(2):
        k, q = core * HEAD_DIM, core * q_width
        wide[:, :HEAD_DIM] = held[:, k_first + k : k_first + k + HEAD_DIM]
        wide[:, HEAD_DIM : 2 * HEAD_DIM] = held[:, v_first + k : v_first + k + HEAD_DIM]
        wide[:, 2 * HEAD_DIM : 2 * HEAD_DIM + q_width] = held[:, q : q + q_width]
        wide[:, 2 * HEAD_DIM + q_width :] = held[:, o_first + q : o_first + q + q_width]
        for tile in range(tiles):
            tall[tile * depth : (tile + 1) * depth, :] = wide[:, tile * LANES : (tile + 1) * LANES]
        piece = tall[...].astype(jnp.bfloat16)

        @pl.when(core_ref[0] == core)
        def _(piece=piece):
            own_ref[...] = piece

        @pl.when(core_ref[0] != core)
        def _(piece=piece):
            other_ref[...] = piece


def copies_kernel(core_ref, own_ref, other_ref, out_ref):
    @pl.when(core_ref[0] == 0)
    def _():
        for to in range(out_ref.shape[0]):
            out_ref[to, 0] = own_ref[...]
            out_ref[to, 1] = other_ref[...]

    @pl.when(core_ref[0] != 0)
    def _():
        for to in range(out_ref.shape[0]):
            out_ref[to, 0] = other_ref[...]
            out_ref[to, 1] = own_ref[...]


def unpack_kernel(depth, in_ref, out_ref, tall, wide):
    for source in range(in_ref.shape[0]):
        tall[...] = in_ref[source].astype(jnp.float32)
        for tile in range(out_ref.shape[1] // LANES):
            wide[source * depth : (source + 1) * depth, tile * LANES : (tile + 1) * LANES] = tall[
                tile * depth : (tile + 1) * depth, :
            ]
    out_ref[...] = wide[...].astype(jnp.bfloat16)


def project_kernel(
    side, unit, core_ref, own_ref, other_ref, signs_ref, gain_ref, w_any,
    kv_ref, qu_ref, wide, hh, weight, sem,
):
    rows, width = wide.shape
    block = 2 * rows
    members = own_ref.shape[0] // rows
    quarter = width // members
    fetch = pltpu.make_async_copy(w_any, weight, sem)
    fetch.start()
    gain = gain_ref[...]
    for half in range(2):
        mine = core_ref[0] == half
        for x in range(members):
            a, b = x * rows, (x + 1) * rows
            held = jnp.where(mine, own_ref[a:b, :].astype(jnp.float32), other_ref[a:b, :].astype(jnp.float32))

            @pl.when(core_ref[0] == 0)
            def _(x=x, held=held):
                wide[:, x * quarter : (x + 1) * quarter] = held[:, :quarter]

            @pl.when(core_ref[0] != 0)
            def _(x=x, held=held):
                for i in range(quarter // unit):
                    y, z = divmod(x * quarter // unit + i, side)
                    to = (z * side + y) * unit
                    wide[:, to : to + unit] = held[:, i * unit : (i + 1) * unit]

        x = wide[...]
        signs = signs_ref[half * rows : (half + 1) * rows, :].astype(jnp.float32)
        inv = lax.rsqrt(jnp.sum(x * x, axis=1, keepdims=True) / width + 1e-06)
        along = jnp.sum(x * signs, axis=1, keepdims=True) / width
        hh[half * rows : (half + 1) * rows, :] = (x * inv * gain).astype(jnp.bfloat16)
        hh[(2 + half) * rows : (3 + half) * rows, :] = (
            (signs * inv - x * (inv * inv * inv * along)) * gain
        ).astype(jnp.bfloat16)
    fetch.wait()
    both = 2 * HEAD_DIM
    q_width = GROUP * HEAD_DIM
    for part in range(2):
        a, b = part * block, (part + 1) * block
        r = jnp.dot(hh[a:b, :], weight[:, : 4 * LANES], preferred_element_type=jnp.float32)
        at = part * HEAD_DIM
        kv_ref[:, at : at + HEAD_DIM] = r[:, :HEAD_DIM].astype(jnp.bfloat16)
        kv_ref[:, both + at : both + at + HEAD_DIM] = r[:, HEAD_DIM:both].astype(jnp.bfloat16)
        qu_ref[a:b, :q_width] = r[:, both : both + q_width].astype(jnp.bfloat16)
    u = jnp.dot(signs_ref[...], weight[:, 3 * LANES :], preferred_element_type=jnp.float32)
    qu_ref[2 * block :, :] = u.astype(jnp.bfloat16)


def attend_kernel(
    rows, side, theirs, core_ref, qu_ref, far, before, here, after, segq_ref, segk_ref, w_any,
    out_ref, share_ref, window, o_ext, weight, flat, w_sem,
):
    block = 2 * rows
    reach = (2 * SPAN + 1) * rows
    core = core_ref[0]
    tile = 1 - core if theirs else core
    o_width = weight.shape[1]
    fetch = pltpu.make_async_copy(w_any.at[:, pl.ds(w_any.shape[1] - o_width, o_width)], weight, w_sem)
    fetch.start()

    @pl.when(tile == 0)
    def _():
        window[0:rows] = far[...]
        window[rows : rows + block] = before[...]
        window[rows + block : rows + 2 * block] = here[...]
        window[rows + 2 * block :] = after[...]

    @pl.when(tile != 0)
    def _():
        window[0:block] = before[...]
        window[block : 2 * block] = here[...]
        window[2 * block : 3 * block] = after[...]
        window[3 * block :] = far[...]

    lo = pl.multiple_of(tile * rows, rows)
    shift = o_width - GROUP * HEAD_DIM
    scale = 1.0 / HEAD_DIM**0.5
    to_exp2 = scale * 1.4426950408889634
    both = 2 * HEAD_DIM
    keys = window[:, :both]
    values = window[:, both:]

    def heads(first):
        held = qu_ref[pl.ds(first + lo, rows), :]
        return jnp.concatenate([held[:, h * HEAD_DIM : (h + 1) * HEAD_DIM] for h in range(GROUP)], axis=0)

    q, q_t = heads(0), heads(block)
    segq = segq_ref[pl.ds(lo, rows), :]
    mask = jnp.concatenate([segq] * GROUP, axis=0) == segk_ref[:, pl.ds(lo, reach)]
    s = lax.dot_general(q, keys[:, :HEAD_DIM], NT, preferred_element_type=jnp.float32)
    s_t = lax.dot_general(jnp.concatenate([q_t, q], axis=1), keys, NT, preferred_element_type=jnp.float32)
    s = jnp.where(mask, s, -1e30)
    e = jnp.exp2((s - jnp.max(s, axis=1, keepdims=True)) * to_exp2)
    inv = 1.0 / jnp.sum(e, axis=1, keepdims=True)
    mean = jnp.sum(e * s_t, axis=1, keepdims=True) * inv
    e_t = (e * ((s_t - mean) * scale)).astype(jnp.bfloat16)
    e = e.astype(jnp.bfloat16)
    made = jnp.dot(e, values, preferred_element_type=jnp.float32)
    out = (made[:, :HEAD_DIM] * inv).astype(jnp.bfloat16)
    out_t = jnp.dot(e_t, values[:, :HEAD_DIM], preferred_element_type=jnp.float32) + made[:, HEAD_DIM:]
    out_t = (out_t * inv).astype(jnp.bfloat16).astype(jnp.float32)
    u = qu_ref[pl.ds(2 * block + lo, rows), :].astype(jnp.float32)
    terms = jnp.zeros((rows, 1), jnp.float32)
    o_ext[:, :shift] = jnp.zeros((rows, shift), jnp.bfloat16)
    for head in range(GROUP):
        a, b = shift + head * HEAD_DIM, shift + (head + 1) * HEAD_DIM
        at = head * rows
        o_ext[:, a:b] = out[at : at + rows]
        terms += jnp.sum(out_t[at : at + rows] * u[:, a:b], axis=1, keepdims=True)
    numbers = lax.broadcasted_iota(jnp.int32, (rows, share_ref.shape[1]), 1)
    share_ref[...] = jnp.sum(jnp.where(segq == numbers, terms, 0.0), axis=0, keepdims=True)
    fetch.wait()
    width = weight.shape[0]
    step, unit = width // 4, width // side**2
    for part in range(4):
        a, b = part * step, (part + 1) * step
        r = lax.dot_general(weight[a:b, :], o_ext[...], NT, preferred_element_type=jnp.float32)

        @pl.when(core == 0)
        def _(a=a, b=b, r=r):
            out_ref[a:b, :] = r.astype(out_ref.dtype)

        @pl.when(core != 0)
        def _(a=a, r=r):
            for i in range(step // unit):
                z, y = divmod(a // unit + i, side)
                to = (y * side + z) * unit
                flat[to : to + unit, :] = r[i * unit : (i + 1) * unit, :]

    @pl.when(core != 0)
    def _():
        out_ref[...] = flat[...].astype(out_ref.dtype)


def body(owned_rows, arrival, image_lengths, probe_seeds, in_gain, w_q, w_kv, w_out):
    bf16, f32 = jnp.bfloat16, jnp.float32
    rows, width = owned_rows.shape
    n_x, n_z, n_seq = lax.axis_size("x"), lax.axis_size("z"), lax.axis_size(SEQ)
    core, member = lax.axis_index("c"), lax.axis_index("x")
    core_word = jnp.reshape(core, (1,)).astype(jnp.int32)
    n_block = lax.axis_size(COLUMN)
    block_index = lax.axis_index(COLUMN)
    quarter = width // n_x
    depth = w_q.shape[0]
    block = 2 * rows
    images = image_lengths.shape[0]
    q_width = GROUP * HEAD_DIM
    columns = 2 * HEAD_DIM + 2 * q_width

    tall_rows = -(-depth * (columns // LANES) // 16) * 16
    piece = jax.ShapeDtypeStruct((tall_rows, LANES), bf16)
    own_piece, other_piece = pl.pallas_call(
        functools.partial(pack_kernel, depth),
        out_shape=(piece, piece),
        in_specs=[SMEM, VMEM],
        out_specs=(VMEM, VMEM),
        scratch_shapes=[pltpu.VMEM((depth, columns), f32), pltpu.VMEM((tall_rows, LANES), f32)],
        compiler_params=params(50),
    )(core_word, jnp.concatenate([w_q, w_kv[:, 0], w_kv[:, 1], w_out.T], axis=1))
    other_piece = lax.ppermute(other_piece, "c", [(0, 1), (1, 0)])
    pieces = pl.pallas_call(
        copies_kernel,
        out_shape=jax.ShapeDtypeStruct((n_z, 2, tall_rows, LANES), bf16),
        in_specs=[SMEM] + [VMEM] * 2,
        out_specs=VMEM,
        compiler_params=params(50),
    )(core_word, own_piece, other_piece)
    side = range(n_z)
    place = lambda y, z, c: (y * n_z + z) * 2 + c
    by_z = [[place(y, z, 0) for z in side] for y in side] + [[place(y, z, 1) for y in side] for z in side]
    by_y = [[place(y, z, 0) for y in side] for z in side] + [[place(y, z, 1) for z in side] for y in side]
    strip = lax.all_to_all(pieces, SEQ, split_axis=0, concat_axis=0, tiled=True, axis_index_groups=by_z)
    strip = strip.reshape(2 * n_z, tall_rows, LANES)
    strip = pl.pallas_call(
        functools.partial(unpack_kernel, depth),
        out_shape=jax.ShapeDtypeStruct((2 * n_z * depth, columns), bf16),
        in_specs=[VMEM],
        out_specs=VMEM,
        scratch_shapes=[pltpu.VMEM((tall_rows, LANES), f32), pltpu.VMEM((2 * n_z * depth, columns), f32)],
        compiler_params=params(50),
    )(strip)
    weights = lax.all_gather(strip, SEQ, axis=0, tiled=True, axis_index_groups=by_y)

    part = lax.dynamic_slice_in_dim(owned_rows, member * quarter, quarter, 1)
    padded = -(-quarter // LANES) * LANES
    part = jnp.pad(part, ((0, 0), (0, padded - quarter))).reshape(rows, 2, padded // 2)
    part, strip = lax.optimization_barrier((part, strip))
    arrived = lax.all_to_all(part, SEQ, split_axis=0, concat_axis=0, tiled=True)
    arrived = jnp.take(arrived.reshape(rows, padded), arrival[0], axis=0, mode="clip")
    own = lax.all_gather(arrived, "x", axis=0, tiled=True)
    own, image_lengths, probe_seeds = lax.optimization_barrier((own, image_lengths, probe_seeds))
    other = lax.ppermute(own, "c", [(0, 1), (1, 0)])

    ends = jnp.cumsum(image_lengths, dtype=jnp.int32)
    starts = ends - image_lengths
    first = block_index * block
    positions = first + jnp.arange(block, dtype=jnp.int32)
    seg = segment_of(positions, ends)
    onehot = seg[:, None] == jnp.arange(images, dtype=jnp.int32)[None, :]
    start_row = jnp.sum(jnp.where(onehot, starts[None, :], 0), axis=1, dtype=jnp.int32)
    seed_row = jnp.sum(jnp.where(onehot, probe_seeds[None, :], 0), axis=1, dtype=jnp.int32)
    unit = 2 * depth
    turned = lambda row: jnp.transpose(row.reshape(n_z, n_z, unit), (1, 0, 2)).reshape(width)
    numbers = jnp.arange(width, dtype=jnp.int32)
    numbers = jnp.where(core == 0, numbers, turned(numbers))
    gain = jnp.where(core == 0, in_gain, turned(in_gain))
    signs = probe_signs(seed_row, positions - start_row, numbers).astype(bf16)
    kpos = first - SPAN * rows + jnp.arange(block + 2 * SPAN * rows, dtype=jnp.int32)
    valid = (kpos >= 0) & (kpos < block * n_block)
    segk = jnp.where(valid, segment_of(kpos, ends), -1)

    kv, qu = pl.pallas_call(
        functools.partial(project_kernel, n_z, unit),
        out_shape=(
            jax.ShapeDtypeStruct((block, 4 * HEAD_DIM), bf16),
            jax.ShapeDtypeStruct((3 * block, 3 * LANES), bf16),
        ),
        in_specs=[SMEM] + [VMEM] * 4 + [ANY],
        out_specs=(VMEM,) * 2,
        scratch_shapes=[
            pltpu.VMEM((rows, width), f32),
            pltpu.VMEM((2 * block, width), bf16),
            pltpu.VMEM((width, columns), bf16),
            pltpu.SemaphoreType.DMA,
        ],
        compiler_params=params(50),
        cost_estimate=pl.CostEstimate(flops=6 * block * width * columns, bytes_accessed=8_000_000, transcendentals=0),
    )(core_word, own, other, signs, gain[None, :], weights)
    before, after = moved(kv, 1), moved(kv, -1)
    ahead = [((b, 1), (b + 2, 1)) for b in range(n_block - 2)] + [((b + 2, 0), (b, 0)) for b in range(n_block - 2)]
    behind = [((b + 2, 1), (b, 1)) for b in range(n_block - 2)] + [((b, 0), (b + 2, 0)) for b in range(n_block - 2)]
    flat_pairs = lambda pairs: [(2 * b + c, 2 * to + d) for (b, c), (to, d) in pairs]
    half = lambda which: lax.dynamic_slice_in_dim(kv, which * rows, rows, 0)
    far_theirs = lax.ppermute(half(core), SEQ, flat_pairs(ahead))
    far_mine = lax.ppermute(half(1 - core), SEQ, flat_pairs(behind))
    segq, segk = seg[:, None], segk[None, :]

    def attend(is_theirs, far):
        return pl.pallas_call(
            functools.partial(attend_kernel, rows, n_z, is_theirs),
            out_shape=(
                jax.ShapeDtypeStruct((width, rows), bf16 if is_theirs else f32),
                jax.ShapeDtypeStruct((1, images), f32),
            ),
            in_specs=[SMEM] + [VMEM] * 7 + [ANY],
            out_specs=(VMEM, VMEM),
            scratch_shapes=[
                pltpu.VMEM((7 * rows, 4 * HEAD_DIM), bf16),
                pltpu.VMEM((rows, 3 * LANES), bf16),
                pltpu.VMEM((width, 3 * LANES), bf16),
                pltpu.VMEM((width, rows), f32),
                pltpu.SemaphoreType.DMA,
            ],
            compiler_params=params(50),
            cost_estimate=pl.CostEstimate(flops=1_000_000_000, bytes_accessed=4_000_000, transcendentals=350_000),
        )(core_word, qu, far, before, kv, after, segq, segk, weights)

    theirs, share_theirs = attend(True, far_theirs)
    theirs, far_mine = lax.optimization_barrier((theirs, far_mine))
    theirs = lax.ppermute(theirs, "c", [(0, 1), (1, 0)])
    mine, share = attend(False, far_mine)
    share = share + share_theirs
    group = (mine + theirs.astype(f32)).astype(bf16)
    velocity = lax.psum_scatter(group, "x", scatter_dimension=0, tiled=True).T
    share, group = lax.optimization_barrier((share, group))
    share = jnp.sum(spread(share[0], ("z", "c")), axis=0)
    divergence = jnp.sum(spread(share, ("y", "x")), axis=0) / width
    return (velocity, divergence)


def solution(mesh):
    n_seq, n_x = mesh.devices.shape
    n_y = 1
    while n_y * n_y * 2 < n_seq:
        n_y *= 2
    devices = mesh.devices.reshape(n_y, n_seq // 2 // n_y, 2, n_x)
    split = Mesh(devices, ("y", "z", "c", "x"))
    in_specs = (
        P(SEQ, None),
        P(SEQ, None),
        P(),
        P(),
        P(),
        P(SEQ, "x"),
        P(SEQ, None, "x"),
        P("x", SEQ),
    )
    out_specs = (P(SEQ, "x"), P())
    return jax.shard_map(body, mesh=split, in_specs=in_specs, out_specs=out_specs, check_vma=False)
```

```python
import functools

import jax
import jax.numpy as jnp
from jax import lax
from jax.experimental import pallas as pl
from jax.experimental.pallas import tpu as pltpu
from jax.sharding import Mesh
from jax.sharding import PartitionSpec as P

HEADS = 24
KV_HEADS = 8
HEAD_DIM = 96
GROUP = HEADS // KV_HEADS
SPAN = 3
SEQ = ("y", "z", "c")
COLUMN = ("y", "z")


def segment_of(pos, ends):
    return jnp.sum((ends[None, :] <= pos[:, None]).astype(jnp.int32), axis=1, dtype=jnp.int32)


def probe_signs(seed_row, local_row, columns):
    mixed = seed_row[:, None] * 40503 + local_row[:, None] * 69069 + columns[None, :] * 2654435
    mixed = mixed ^ jnp.right_shift(mixed, 15)
    mixed = mixed * 1597334677
    mixed = mixed ^ jnp.right_shift(mixed, 13)
    mixed = mixed * 668265263
    bit = jnp.right_shift(mixed, 11) & 1
    return (1 - 2 * bit).astype(jnp.float32)


def spread(array, axes):
    count = lax.axis_size(axes)
    copies = jnp.broadcast_to(array[None], (count,) + array.shape)
    return lax.all_to_all(copies, axes, split_axis=0, concat_axis=0, tiled=True)


def moved(array, by):
    count = lax.axis_size(COLUMN)
    pairs = [(i, i + by) for i in range(count) if 0 <= i + by < count]
    return lax.ppermute(array, COLUMN, pairs)


NT = (((1,), (1,)), ((), ()))
VMEM = pl.BlockSpec(memory_space=pltpu.VMEM)
SMEM = pl.BlockSpec(memory_space=pltpu.SMEM)
ANY = pl.BlockSpec(memory_space=pl.ANY)
LANES = 128


def params(mib):
    return pltpu.CompilerParams(vmem_limit_bytes=mib * 1024 * 1024)


def pack_kernel(depth, core_ref, in_ref, own_ref, other_ref, wide, tall):
    q_width = GROUP * HEAD_DIM
    tiles = wide.shape[1] // LANES
    k_first = 2 * q_width
    v_first = k_first + 2 * HEAD_DIM
    o_first = v_first + 2 * HEAD_DIM
    held = in_ref[...].astype(jnp.float32)
    tall[...] = jnp.zeros_like(tall)
    for core in range(2):
        k, q = core * HEAD_DIM, core * q_width
        wide[:, :HEAD_DIM] = held[:, k_first + k : k_first + k + HEAD_DIM]
        wide[:, HEAD_DIM : 2 * HEAD_DIM] = held[:, v_first + k : v_first + k + HEAD_DIM]
        wide[:, 2 * HEAD_DIM : 2 * HEAD_DIM + q_width] = held[:, q : q + q_width]
        wide[:, 2 * HEAD_DIM + q_width :] = held[:, o_first + q : o_first + q + q_width]
        for tile in range(tiles):
            tall[tile * depth : (tile + 1) * depth, :] = wide[:, tile * LANES : (tile + 1) * LANES]
        piece = tall[...].astype(jnp.bfloat16)

        @pl.when(core_ref[0] == core)
        def _(piece=piece):
            own_ref[...] = piece

        @pl.when(core_ref[0] != core)
        def _(piece=piece):
            other_ref[...] = piece


def copies_kernel(core_ref, own_ref, other_ref, out_ref):
    @pl.when(core_ref[0] == 0)
    def _():
        for to in range(out_ref.shape[0]):
            out_ref[to, 0] = own_ref[...]
            out_ref[to, 1] = other_ref[...]

    @pl.when(core_ref[0] != 0)
    def _():
        for to in range(out_ref.shape[0]):
            out_ref[to, 0] = other_ref[...]
            out_ref[to, 1] = own_ref[...]


def unpack_kernel(depth, in_ref, out_ref, tall, wide):
    for source in range(in_ref.shape[0]):
        tall[...] = in_ref[source].astype(jnp.float32)
        for tile in range(out_ref.shape[1] // LANES):
            wide[source * depth : (source + 1) * depth, tile * LANES : (tile + 1) * LANES] = tall[
                tile * depth : (tile + 1) * depth, :
            ]
    out_ref[...] = wide[...].astype(jnp.bfloat16)


def project_kernel(
    side, unit, core_ref, own_ref, other_ref, signs_ref, gain_ref, w_any,
    kv_ref, qu_ref, wide, hh, weight, sem,
):
    rows, width = wide.shape
    block = 2 * rows
    members = own_ref.shape[0] // rows
    quarter = width // members
    fetch = pltpu.make_async_copy(w_any, weight, sem)
    fetch.start()
    gain = gain_ref[...]
    for half in range(2):
        mine = core_ref[0] == half
        for x in range(members):
            a, b = x * rows, (x + 1) * rows
            held = jnp.where(mine, own_ref[a:b, :].astype(jnp.float32), other_ref[a:b, :].astype(jnp.float32))

            @pl.when(core_ref[0] == 0)
            def _(x=x, held=held):
                wide[:, x * quarter : (x + 1) * quarter] = held[:, :quarter]

            @pl.when(core_ref[0] != 0)
            def _(x=x, held=held):
                for i in range(quarter // unit):
                    y, z = divmod(x * quarter // unit + i, side)
                    to = (z * side + y) * unit
                    wide[:, to : to + unit] = held[:, i * unit : (i + 1) * unit]

        x = wide[...]
        signs = signs_ref[half * rows : (half + 1) * rows, :].astype(jnp.float32)
        inv = lax.rsqrt(jnp.sum(x * x, axis=1, keepdims=True) / width + 1e-06)
        along = jnp.sum(x * signs, axis=1, keepdims=True) / width
        hh[half * rows : (half + 1) * rows, :] = (x * inv * gain).astype(jnp.bfloat16)
        hh[(2 + half) * rows : (3 + half) * rows, :] = (
            (signs * inv - x * (inv * inv * inv * along)) * gain
        ).astype(jnp.bfloat16)
    fetch.wait()
    both = 2 * HEAD_DIM
    q_width = GROUP * HEAD_DIM
    for part in range(2):
        a, b = part * block, (part + 1) * block
        r = jnp.dot(hh[a:b, :], weight[:, : 4 * LANES], preferred_element_type=jnp.float32)
        at = part * HEAD_DIM
        kv_ref[:, at : at + HEAD_DIM] = r[:, :HEAD_DIM].astype(jnp.bfloat16)
        kv_ref[:, both + at : both + at + HEAD_DIM] = r[:, HEAD_DIM:both].astype(jnp.bfloat16)
        qu_ref[a:b, :q_width] = r[:, both : both + q_width].astype(jnp.bfloat16)
    u = jnp.dot(signs_ref[...], weight[:, 3 * LANES :], preferred_element_type=jnp.float32)
    qu_ref[2 * block :, :] = u.astype(jnp.bfloat16)


def attend_kernel(
    rows, side, theirs, core_ref, qu_ref, far, before, here, after, segq_ref, segk_ref, w_any,
    out_ref, share_ref, window, o_ext, weight, flat, w_sem,
):
    block = 2 * rows
    reach = (2 * SPAN + 1) * rows
    core = core_ref[0]
    tile = 1 - core if theirs else core
    o_width = weight.shape[1]
    fetch = pltpu.make_async_copy(w_any.at[:, pl.ds(w_any.shape[1] - o_width, o_width)], weight, w_sem)
    fetch.start()

    @pl.when(tile == 0)
    def _():
        window[0:rows] = far[...]
        window[rows : rows + block] = before[...]
        window[rows + block : rows + 2 * block] = here[...]
        window[rows + 2 * block :] = after[...]

    @pl.when(tile != 0)
    def _():
        window[0:block] = before[...]
        window[block : 2 * block] = here[...]
        window[2 * block : 3 * block] = after[...]
        window[3 * block :] = far[...]

    lo = pl.multiple_of(tile * rows, rows)
    shift = o_width - GROUP * HEAD_DIM
    scale = 1.0 / HEAD_DIM**0.5
    to_exp2 = scale * 1.4426950408889634
    both = 2 * HEAD_DIM
    keys = window[:, :both]
    values = window[:, both:]

    def heads(first):
        held = qu_ref[pl.ds(first + lo, rows), :]
        return jnp.concatenate([held[:, h * HEAD_DIM : (h + 1) * HEAD_DIM] for h in range(GROUP)], axis=0)

    q, q_t = heads(0), heads(block)
    segq = segq_ref[pl.ds(lo, rows), :]
    mask = jnp.concatenate([segq] * GROUP, axis=0) == segk_ref[:, pl.ds(lo, reach)]
    s = lax.dot_general(q, keys[:, :HEAD_DIM], NT, preferred_element_type=jnp.float32)
    s_t = lax.dot_general(jnp.concatenate([q_t, q], axis=1), keys, NT, preferred_element_type=jnp.float32)
    s = jnp.where(mask, s, -1e30)
    e = jnp.exp2((s - jnp.max(s, axis=1, keepdims=True)) * to_exp2)
    inv = 1.0 / jnp.sum(e, axis=1, keepdims=True)
    mean = jnp.sum(e * s_t, axis=1, keepdims=True) * inv
    e_t = (e * ((s_t - mean) * scale)).astype(jnp.bfloat16)
    e = e.astype(jnp.bfloat16)
    made = jnp.dot(e, values, preferred_element_type=jnp.float32)
    out = (made[:, :HEAD_DIM] * inv).astype(jnp.bfloat16)
    out_t = jnp.dot(e_t, values[:, :HEAD_DIM], preferred_element_type=jnp.float32) + made[:, HEAD_DIM:]
    out_t = (out_t * inv).astype(jnp.bfloat16).astype(jnp.float32)
    u = qu_ref[pl.ds(2 * block + lo, rows), :].astype(jnp.float32)
    terms = jnp.zeros((rows, 1), jnp.float32)
    o_ext[:, :shift] = jnp.zeros((rows, shift), jnp.bfloat16)
    for head in range(GROUP):
        a, b = shift + head * HEAD_DIM, shift + (head + 1) * HEAD_DIM
        at = head * rows
        o_ext[:, a:b] = out[at : at + rows]
        terms += jnp.sum(out_t[at : at + rows] * u[:, a:b], axis=1, keepdims=True)
    numbers = lax.broadcasted_iota(jnp.int32, (rows, share_ref.shape[1]), 1)
    share_ref[...] = jnp.sum(jnp.where(segq == numbers, terms, 0.0), axis=0, keepdims=True)
    fetch.wait()
    width = weight.shape[0]
    step, unit = width // 4, width // side**2
    for part in range(4):
        a, b = part * step, (part + 1) * step
        r = lax.dot_general(weight[a:b, :], o_ext[...], NT, preferred_element_type=jnp.float32)

        @pl.when(core == 0)
        def _(a=a, b=b, r=r):
            out_ref[a:b, :] = r.astype(out_ref.dtype)

        @pl.when(core != 0)
        def _(a=a, r=r):
            for i in range(step // unit):
                z, y = divmod(a // unit + i, side)
                to = (y * side + z) * unit
                flat[to : to + unit, :] = r[i * unit : (i + 1) * unit, :]

    @pl.when(core != 0)
    def _():
        out_ref[...] = flat[...].astype(out_ref.dtype)


def body(owned_rows, arrival, image_lengths, probe_seeds, in_gain, w_q, w_kv, w_out):
    bf16, f32 = jnp.bfloat16, jnp.float32
    rows, width = owned_rows.shape
    n_x, n_z, n_seq = lax.axis_size("x"), lax.axis_size("z"), lax.axis_size(SEQ)
    core, member = lax.axis_index("c"), lax.axis_index("x")
    core_word = jnp.reshape(core, (1,)).astype(jnp.int32)
    n_block = lax.axis_size(COLUMN)
    block_index = lax.axis_index(COLUMN)
    quarter = width // n_x
    depth = w_q.shape[0]
    block = 2 * rows
    images = image_lengths.shape[0]
    q_width = GROUP * HEAD_DIM
    columns = 2 * HEAD_DIM + 2 * q_width

    tall_rows = -(-depth * (columns // LANES) // 16) * 16
    piece = jax.ShapeDtypeStruct((tall_rows, LANES), bf16)
    own_piece, other_piece = pl.pallas_call(
        functools.partial(pack_kernel, depth),
        out_shape=(piece, piece),
        in_specs=[SMEM, VMEM],
        out_specs=(VMEM, VMEM),
        scratch_shapes=[pltpu.VMEM((depth, columns), f32), pltpu.VMEM((tall_rows, LANES), f32)],
        compiler_params=params(50),
    )(core_word, jnp.concatenate([w_q, w_kv[:, 0], w_kv[:, 1], w_out.T], axis=1))
    other_piece = lax.ppermute(other_piece, "c", [(0, 1), (1, 0)])
    pieces = pl.pallas_call(
        copies_kernel,
        out_shape=jax.ShapeDtypeStruct((n_z, 2, tall_rows, LANES), bf16),
        in_specs=[SMEM] + [VMEM] * 2,
        out_specs=VMEM,
        compiler_params=params(50),
    )(core_word, own_piece, other_piece)
    part = lax.dynamic_slice_in_dim(owned_rows, member * quarter, quarter, 1)
    padded = -(-quarter // LANES) * LANES
    part = jnp.pad(part, ((0, 0), (0, padded - quarter))).reshape(rows, 2, padded // 2)
    part, pieces = lax.optimization_barrier((part, pieces))
    side = range(n_z)
    place = lambda y, z, c: (y * n_z + z) * 2 + c
    by_z = [[place(y, z, 0) for z in side] for y in side] + [[place(y, z, 1) for y in side] for z in side]
    by_y = [[place(y, z, 0) for y in side] for z in side] + [[place(y, z, 1) for z in side] for y in side]
    strip = lax.all_to_all(pieces, SEQ, split_axis=0, concat_axis=0, tiled=True, axis_index_groups=by_z)
    strip = strip.reshape(2 * n_z, tall_rows, LANES)
    strip = pl.pallas_call(
        functools.partial(unpack_kernel, depth),
        out_shape=jax.ShapeDtypeStruct((2 * n_z * depth, columns), bf16),
        in_specs=[VMEM],
        out_specs=VMEM,
        scratch_shapes=[pltpu.VMEM((tall_rows, LANES), f32), pltpu.VMEM((2 * n_z * depth, columns), f32)],
        compiler_params=params(50),
    )(strip)
    weights = lax.all_gather(strip, SEQ, axis=0, tiled=True, axis_index_groups=by_y)

    arrived = lax.all_to_all(part, SEQ, split_axis=0, concat_axis=0, tiled=True)
    arrived = jnp.take(arrived.reshape(rows, padded), arrival[0], axis=0, mode="clip")
    own = lax.all_gather(arrived, "x", axis=0, tiled=True)
    own, image_lengths, probe_seeds, in_gain = lax.optimization_barrier(
        (own, image_lengths, probe_seeds, in_gain)
    )
    other = lax.ppermute(own, "c", [(0, 1), (1, 0)])

    ends = jnp.cumsum(image_lengths, dtype=jnp.int32)
    starts = ends - image_lengths
    first = block_index * block
    positions = first + jnp.arange(block, dtype=jnp.int32)
    seg = segment_of(positions, ends)
    onehot = seg[:, None] == jnp.arange(images, dtype=jnp.int32)[None, :]
    start_row = jnp.sum(jnp.where(onehot, starts[None, :], 0), axis=1, dtype=jnp.int32)
    seed_row = jnp.sum(jnp.where(onehot, probe_seeds[None, :], 0), axis=1, dtype=jnp.int32)
    unit = 2 * depth
    turned = lambda row: jnp.transpose(row.reshape(n_z, n_z, unit), (1, 0, 2)).reshape(width)
    numbers = jnp.arange(width, dtype=jnp.int32)
    numbers = jnp.where(core == 0, numbers, turned(numbers))
    gain = jnp.where(core == 0, in_gain, turned(in_gain))
    signs = probe_signs(seed_row, positions - start_row, numbers).astype(bf16)
    kpos = first - SPAN * rows + jnp.arange(block + 2 * SPAN * rows, dtype=jnp.int32)
    valid = (kpos >= 0) & (kpos < block * n_block)
    segk = jnp.where(valid, segment_of(kpos, ends), -1)

    kv, qu = pl.pallas_call(
        functools.partial(project_kernel, n_z, unit),
        out_shape=(
            jax.ShapeDtypeStruct((block, 4 * HEAD_DIM), bf16),
            jax.ShapeDtypeStruct((3 * block, 3 * LANES), bf16),
        ),
        in_specs=[SMEM] + [VMEM] * 4 + [ANY],
        out_specs=(VMEM,) * 2,
        scratch_shapes=[
            pltpu.VMEM((rows, width), f32),
            pltpu.VMEM((2 * block, width), bf16),
            pltpu.VMEM((width, columns), bf16),
            pltpu.SemaphoreType.DMA,
        ],
        compiler_params=params(50),
        cost_estimate=pl.CostEstimate(flops=6 * block * width * columns, bytes_accessed=8_000_000, transcendentals=0),
    )(core_word, own, other, signs, gain[None, :], weights)
    before, after = moved(kv, 1), moved(kv, -1)
    ahead = [((b, 1), (b + 2, 1)) for b in range(n_block - 2)] + [((b + 2, 0), (b, 0)) for b in range(n_block - 2)]
    behind = [((b + 2, 1), (b, 1)) for b in range(n_block - 2)] + [((b, 0), (b + 2, 0)) for b in range(n_block - 2)]
    flat_pairs = lambda pairs: [(2 * b + c, 2 * to + d) for (b, c), (to, d) in pairs]
    half = lambda which: lax.dynamic_slice_in_dim(kv, which * rows, rows, 0)
    far_theirs = lax.ppermute(half(core), SEQ, flat_pairs(ahead))
    far_mine = lax.ppermute(half(1 - core), SEQ, flat_pairs(behind))
    segq, segk = seg[:, None], segk[None, :]

    def attend(is_theirs, far):
        return pl.pallas_call(
            functools.partial(attend_kernel, rows, n_z, is_theirs),
            out_shape=(
                jax.ShapeDtypeStruct((width, rows), bf16),
                jax.ShapeDtypeStruct((1, images), f32),
            ),
            in_specs=[SMEM] + [VMEM] * 7 + [ANY],
            out_specs=(VMEM, VMEM),
            scratch_shapes=[
                pltpu.VMEM((7 * rows, 4 * HEAD_DIM), bf16),
                pltpu.VMEM((rows, 3 * LANES), bf16),
                pltpu.VMEM((width, 3 * LANES), bf16),
                pltpu.VMEM((width, rows), f32),
                pltpu.SemaphoreType.DMA,
            ],
            compiler_params=params(50),
            cost_estimate=pl.CostEstimate(flops=1_000_000_000, bytes_accessed=4_000_000, transcendentals=350_000),
        )(core_word, qu, far, before, kv, after, segq, segk, weights)

    theirs, share_theirs = attend(True, far_theirs)
    theirs, far_mine = lax.optimization_barrier((theirs, far_mine))
    theirs = lax.ppermute(theirs, "c", [(0, 1), (1, 0)])
    mine, share = attend(False, far_mine)
    share = share + share_theirs
    group = (mine.astype(f32) + theirs.astype(f32)).astype(bf16)
    velocity = lax.psum_scatter(group, "x", scatter_dimension=0, tiled=True).T
    share, group = lax.optimization_barrier((share, group))
    share = jnp.sum(spread(share[0], ("z", "c")), axis=0)
    divergence = jnp.sum(spread(share, ("y", "x")), axis=0) / width
    return (velocity, divergence)


def solution(mesh):
    n_seq, n_x = mesh.devices.shape
    n_y = 1
    while n_y * n_y * 2 < n_seq:
        n_y *= 2
    devices = mesh.devices.reshape(n_y, n_seq // 2 // n_y, 2, n_x)
    split = Mesh(devices, ("y", "z", "c", "x"))
    in_specs = (
        P(SEQ, None),
        P(SEQ, None),
        P(),
        P(),
        P(),
        P(SEQ, "x"),
        P(SEQ, None, "x"),
        P("x", SEQ),
    )
    out_specs = (P(SEQ, "x"), P())
    return jax.shard_map(body, mesh=split, in_specs=in_specs, out_specs=out_specs, check_vma=False)
```
